32 devices in a mesh: seq: 8 (over z, y), mp: 4 (over x, core).
Axes of the slice: x: 2, y: 2, z: 4, core: 2. Of those that a mesh axis runs over, the one named last changes fastest.
Arguments:
- inputs: bfloat16 [4, 4, 2048], replicated, may hold values from -3 to 3
- w_qkv: bfloat16 [3, 2048, 2048], P(None, None, 'mp'), may hold values from -0.125 to 0.125
- w_out: bfloat16 [2048, 2048], P('mp'), may hold values from -0.125 to 0.125
- w_gate_up: bfloat16 [2, 2048, 4096], P(None, None, 'mp'), may hold values from -0.125 to 0.125
- w_down: bfloat16 [4096, 2048], P('mp'), may hold values from -0.09375 to 0.09375
- cache_keys: bfloat16 [4, 1024, 2048], P(None, 'seq', 'mp'), may hold values from -256 to 256
- cache_values: bfloat16 [4, 1024, 2048], P(None, 'seq', 'mp'), may hold values from -6 to 6
- lengths: int32 [4], replicated, may hold values from 1 to 1024, as said below
Outputs:
- hidden: bfloat16 [4, 4, 2048], P(None, None, 'mp')
- queries: bfloat16 [4, 4, 2048], P(None, None, 'mp')
- new_keys: bfloat16 [4, 4, 2048], P(None, None, 'mp')
- new_values: bfloat16 [4, 4, 2048], P(None, None, 'mp')
The draws below stay inside these ranges and needn't reach their ends.
Inputs may be any that keep to these rules, and one draw needn't show every extreme that they name: `lengths`: half of the 4 requests hold 1 to 64 cached positions, the others 1024 - 1024 // 8 to 1024; one request holds exactly 1024.
All inputs are finite; a program needn't handle non-finite values.
Results may differ from the reference program's by a relative error of at most 0.015.
The reference program's roundings to bfloat16 on the way count: a program that leaves them out, or rounds other values in their place, can miss the bound.
Values may be sent and summed in bfloat16 or wider, within the bound.
A program may use at most 128 MiB of HBM per device.

```python
import jax
import jax.numpy as jnp
from jax import lax

D = 2048
H = 16
DH = 128
FF = 4096
STEPS = 4
REQS = 4
CACHE = 1024


def draw_cache_keys(key, part):
    normal_key = jax.random.fold_in(key, 0)
    full_shape = (REQS, CACHE, H * DH)
    return jnp.clip(2.5 * jax.random.normal(normal_key, full_shape, jnp.float32), -15.0, 15.0).astype(jnp.bfloat16)


def draw_lengths(key, part):
    short_key, long_key, order_key = jax.random.split(key, 3)
    short_lens = jax.random.randint(short_key, (REQS,), 1, CACHE // 16 + 1)
    long_lens = jax.random.randint(long_key, (REQS,), CACHE - CACHE // 8, CACHE + 1)
    ranking = jax.random.permutation(order_key, REQS)
    chosen = jnp.where(ranking < REQS // 2, long_lens, short_lens)
    return jnp.where(ranking == 0, CACHE, chosen).astype(jnp.int32)


def steps_of(rng, dims, shards, smallest, top_value):
    level, own = 1.0, jax.random.fold_in(rng, 6)
    for position, shards_of in shards:
        heights = jnp.exp(jax.random.uniform(jax.random.fold_in(own, position), (shards_of,), jnp.float32, smallest / len(shards), top_value / len(shards)))
        level = level * jnp.repeat(heights, dims[position] // shards_of).reshape([-1 if axis == position else 1 for axis in range(len(dims))])
    return level


def scatter_about(key, extent, deviation, reach, cuts=(), kind=jnp.bfloat16):
    drawn = deviation * jax.random.normal(key, extent, jnp.float32)
    if cuts:
        drawn = drawn * steps_of(key, extent, cuts, -0.22, 0.18)
    return jnp.clip(drawn, -reach, reach).astype(kind)


def setup_inputs(seed: int = 0) -> dict:
    key_list = jax.random.split(jax.random.key(seed), 9)
    inputs = scatter_about(key_list[0], (REQS, STEPS, D), 0.5, 3.0)
    w_qkv = scatter_about(key_list[1], (3, D, H * DH), D ** -0.5, 0.125, ((2, 4),))
    w_out = scatter_about(key_list[2], (H * DH, D), (H * DH) ** -0.5, 0.125, ((0, 4),))
    w_gate_up = scatter_about(key_list[3], (2, D, FF), D ** -0.5, 0.125, ((2, 4),))
    w_down = scatter_about(key_list[4], (FF, D), FF ** -0.5, 0.09375, ((0, 4),))
    cache_keys = draw_cache_keys(jax.random.fold_in(key_list[8], 71), 0)
    cache_values = scatter_about(key_list[6], (REQS, CACHE, H * DH), 1.0, 6.0, ((1, 8), (2, 4)))
    lengths = draw_lengths(jax.random.fold_in(key_list[8], 71), 0)
    return dict(inputs=inputs, w_qkv=w_qkv, w_out=w_out, w_gate_up=w_gate_up, w_down=w_down, cache_keys=cache_keys, cache_values=cache_values, lengths=lengths)


neg_fill = -1e+30
norm_eps = 1e-05
rope_base = 10000.0

def layer_norm(values):
    average = lax.optimization_barrier(jnp.mean(values, axis=-1, keepdims=True))
    centred = values - average
    variance = lax.optimization_barrier(jnp.mean(centred * centred, axis=-1, keepdims=True))
    return centred * lax.rsqrt(variance + norm_eps)

def rotate(values, positions):
    head_dim = values.shape[-1]
    half_dim = head_dim // 2
    inverse = rope_base ** (-2.0 * jnp.arange(half_dim, dtype=jnp.float32) / head_dim)
    angles = positions.astype(jnp.float32)[..., None] * inverse
    angles = jnp.concatenate([angles, angles], axis=-1)[..., None, :]
    turned = jnp.concatenate([-values[..., half_dim:], values[..., :half_dim]], axis=-1)
    return values * jnp.cos(angles) + turned * jnp.sin(angles)

def project(inputs, w_qkv, lengths):
    batch_rows, step_count, model_width = inputs.shape
    normed = layer_norm(inputs.astype(jnp.float32)).astype(jnp.bfloat16)
    flat_rows = normed.reshape(batch_rows * step_count, model_width)
    triple = jnp.einsum('rd,jdk->jrk', flat_rows.astype(jnp.float32), w_qkv.astype(jnp.float32))
    triple = triple.reshape(3, batch_rows, step_count, -1, DH)
    positions = lengths[:, None] + jnp.arange(step_count, dtype=jnp.int32)[None, :]
    queries = rotate(triple[0], positions).astype(jnp.bfloat16)
    new_keys = rotate(triple[1], positions).astype(jnp.bfloat16)
    return (queries, new_keys, triple[2].astype(jnp.bfloat16))

def reference(inputs, w_qkv, w_out, w_gate_up, w_down, cache_keys, cache_values, lengths):
    batch_rows, step_count, model_width = inputs.shape
    queries, new_keys, new_values = project(inputs, w_qkv, lengths)
    head_count = queries.shape[2]
    step_ids = jnp.arange(step_count, dtype=jnp.int32)
    places = jnp.arange(CACHE + step_count, dtype=jnp.int32)

    def one_request(packed):
        query_rows, keys_old, values_old, keys_new, values_new, length_now = packed
        keys_all = jnp.concatenate([keys_old.reshape(CACHE, head_count, DH), keys_new], axis=0).astype(jnp.float32)
        values_all = jnp.concatenate([values_old.reshape(CACHE, head_count, DH), values_new], axis=0).astype(jnp.float32)
        scores = jnp.einsum('thd,khd->thk', query_rows.astype(jnp.float32), keys_all) * DH ** (-0.5)
        live = jnp.where(places[None, :] < CACHE, places[None, :] < length_now, places[None, :] - CACHE <= step_ids[:, None])[:, None, :]
        highest = lax.optimization_barrier(jnp.max(jnp.where(live, scores, neg_fill), axis=-1))
        weights = jnp.where(live, jnp.exp(scores - highest[..., None]), 0.0)
        totals = lax.optimization_barrier(jnp.sum(weights, axis=-1))
        rounded = lax.optimization_barrier(weights.astype(jnp.bfloat16)).astype(jnp.float32)
        summed = jnp.einsum('thk,khd->thd', rounded, values_all)
        return (summed / totals[..., None]).astype(jnp.bfloat16).reshape(step_count, head_count * DH)
    context = lax.map(one_request, (queries, cache_keys, cache_values, new_keys, new_values, lengths))
    flat_count = batch_rows * step_count
    middle = inputs.reshape(flat_count, model_width).astype(jnp.float32) + jnp.dot(context.reshape(flat_count, -1), w_out, preferred_element_type=jnp.float32)
    normed = layer_norm(middle).astype(jnp.bfloat16)
    gate_up = jnp.einsum('rd,jdf->jrf', normed.astype(jnp.float32), w_gate_up.astype(jnp.float32))
    active = (jax.nn.silu(gate_up[0]) * gate_up[1]).astype(jnp.bfloat16)
    hidden = (middle + jnp.dot(active, w_down, preferred_element_type=jnp.float32)).astype(jnp.bfloat16)
    head_width = head_count * DH
    return (hidden.reshape(batch_rows, step_count, model_width), queries.reshape(batch_rows, step_count, head_width), new_keys.reshape(batch_rows, step_count, head_width), new_values.reshape(batch_rows, step_count, head_width))
```

```python
import functools

import jax
import jax.numpy as jnp
from jax import lax
from jax.experimental import pallas as pl
from jax.experimental.pallas import tpu as pltpu
from jax.sharding import PartitionSpec as P

DH = 128
NEG = -1e30
EPS = 1e-05
BASE = 10000.0
MESH = pl.DeviceIdType.MESH
F32 = jnp.float32
BF16 = jnp.bfloat16
QKV_CUTS = 4


def each(count, body):
    if count <= 8:
        for i in range(count):
            body(i)
    else:
        lax.fori_loop(0, count, lambda i, c: (body(i), c)[1], 0)


def iota(shape, axis):
    return lax.broadcasted_iota(jnp.int32, shape, axis)


def layer_norm(values):
    average = jnp.mean(values, axis=-1, keepdims=True)
    centred = values - average
    variance = jnp.mean(centred * centred, axis=-1, keepdims=True)
    return centred * lax.rsqrt(variance + EPS)


def dot(a, b):
    return jnp.dot(a, b, preferred_element_type=F32)


def kernel(
    S, M,
    len_ref, x_hbm, tab_hbm, wqkv_hbm, wout_hbm, wgu_hbm, wdown_hbm, ck_hbm, cv_hbm,
    q_out, k_out, v_out, h_out,
    x_in, tab, wqkv, wout, wgu, wdown, ck, cv,
    xf, send1, recv1, send2, recv2, send3, recv3, mids, send4, recv4,
    xsem, qsem, wsem, csem, s1, r1, s2, r2, s3, r3, s4, r4,
):
    batch, steps, width = x_in.shape
    rows = batch * steps
    block = ck.shape[1]
    cols = wqkv.shape[2]
    heads = cols // DH
    own = rows // S
    pack = own * heads
    me = lax.axis_index("seq")
    mp = lax.axis_index("mp")

    x_copy = pltpu.make_async_copy(x_hbm, x_in, xsem.at[0])
    t_copy = pltpu.make_async_copy(tab_hbm, tab, xsem.at[1])
    x_copy.start()
    t_copy.start()
    cut = width // QKV_CUTS
    q_copies = [
        [
            pltpu.make_async_copy(
                wqkv_hbm.at[j, pl.ds(c * cut, cut)], wqkv.at[j, pl.ds(c * cut, cut)], qsem.at[j, c]
            )
            for c in range(QKV_CUTS)
        ]
        for j in range(3)
    ]
    for j in range(3):
        for c in range(QKV_CUTS):
            q_copies[j][c].start()
    ck_copy = pltpu.make_async_copy(ck_hbm, ck, csem.at[0])
    cv_copy = pltpu.make_async_copy(cv_hbm, cv, csem.at[1])
    ck_copy.start()
    cv_copy.start()
    out_copy = pltpu.make_async_copy(wout_hbm, wout, wsem.at[0])
    gate_copy = pltpu.make_async_copy(wgu_hbm.at[0], wgu.at[0], wsem.at[1])
    up_copy = pltpu.make_async_copy(wgu_hbm.at[1], wgu.at[1], wsem.at[2])
    down_copy = pltpu.make_async_copy(wdown_hbm, wdown, wsem.at[3])

    barrier = pltpu.get_barrier_semaphore()

    def greet_seq(o):
        pl.semaphore_signal(
            barrier, inc=1, device_id={"seq": lax.rem(me + 1 + o, S)}, device_id_type=MESH
        )

    def greet_mp(o):
        pl.semaphore_signal(
            barrier, inc=1, device_id={"mp": lax.rem(mp + 1 + o, M)}, device_id_type=MESH
        )

    each(S - 1, greet_seq)
    each(M - 1, greet_mp)

    x_copy.wait()
    for r in range(batch):
        xf[r * steps : (r + 1) * steps, :] = x_in[r].astype(F32)
    x = xf[...]
    normed = layer_norm(x).astype(BF16)

    def project(j):
        total = None
        for c in range(QKV_CUTS):
            q_copies[j][c].wait()
            term = dot(normed[:, c * cut : (c + 1) * cut], wqkv[j, c * cut : (c + 1) * cut, :])
            total = term if total is None else total + term
        return total

    def rope(values, ref):
        for h in range(heads):
            v = values[:, h * DH : (h + 1) * DH]
            turned = pltpu.roll(v, DH // 2, 1)
            ref[:, h * DH : (h + 1) * DH] = (v * tab[0] + turned * tab[1]).astype(BF16).astype(F32)

    queries = project(0)
    out_copy.start()
    t_copy.wait()
    rope(queries, q_out)

    full = rows * heads
    spread = (iota((full, rows), 0) // heads == iota((full, rows), 1)).astype(F32).astype(BF16)
    wide = dot(spread, q_out[...].astype(BF16))
    own_cols = iota((full, cols), 1) // DH == lax.rem(iota((full, cols), 0), heads)
    wide = jnp.where(own_cols, wide, 0.0).astype(BF16)

    keys = project(1)
    gate_copy.start()
    rope(keys, k_out)
    values = project(2)
    up_copy.start()
    down_copy.start()
    v_out[...] = values.astype(BF16).astype(F32)

    nt = (((1,), (1,)), ((), ()))
    scale = DH ** -0.5
    group = steps * heads
    ck_copy.wait()
    parts = []
    for r in range(batch):
        raw = lax.dot_general(
            wide[r * group : (r + 1) * group], ck[r], nt, preferred_element_type=F32
        )
        place = iota((group, block), 1) + me * block
        parts.append(jnp.where(place < len_ref[r], raw * scale, NEG))
    scores = jnp.concatenate(parts, axis=0)
    fresh = lax.dot_general(wide, k_out[...].astype(BF16), nt, preferred_element_type=F32) * scale
    row, col = iota((full, rows), 0), iota((full, rows), 1)
    live = (
        (row // group == col // steps)
        & (lax.rem(col, steps) <= lax.rem(row // heads, steps))
        & (row // pack == me)
    )
    fresh = jnp.where(live, fresh, NEG)
    top = jnp.maximum(
        jnp.max(scores, axis=1, keepdims=True), jnp.max(fresh, axis=1, keepdims=True)
    )
    weights = jnp.where(scores > 0.5 * NEG, jnp.exp(scores - top), 0.0)
    fresh_w = jnp.where(live, jnp.exp(fresh - top), 0.0)
    total = jnp.sum(weights, axis=1, keepdims=True) + jnp.sum(fresh_w, axis=1, keepdims=True)
    cv_copy.wait()
    weights = weights.astype(BF16)
    summed = jnp.concatenate(
        [dot(weights[r * group : (r + 1) * group], cv[r]) for r in range(batch)], axis=0
    )
    summed = summed + dot(fresh_w.astype(BF16), v_out[...].astype(BF16))
    head_of = lax.rem(iota((full, DH), 0), heads)
    mine = jnp.zeros((full, DH), F32)
    for h in range(heads):
        mine = mine + jnp.where(head_of == h, summed[:, h * DH : (h + 1) * DH], 0.0)
    stats = jnp.where(iota((full, DH), 1) < DH // 2, top, total)
    send1[:, :, :DH] = mine.reshape(S, pack, DH)
    send1[:, :, DH:] = stats.reshape(S, pack, DH)

    pl.semaphore_wait(barrier, S + M - 2)

    def copy1(peer):
        return pltpu.make_async_remote_copy(
            send1.at[peer], recv1.at[me], s1.at[peer], r1.at[me],
            device_id={"seq": peer}, device_id_type=MESH,
        )

    def came(buf, src, send_sem, recv_sem, slot, axis):
        return pltpu.make_async_remote_copy(
            src, buf.at[slot], send_sem, recv_sem.at[slot],
            device_id={axis: slot}, device_id_type=MESH,
        )

    each(S - 1, lambda o: copy1(lax.rem(me + 1 + o, S)).start())
    recv1[me] = send1[me]

    def wait1(o):
        peer = lax.rem(me + 1 + o, S)
        came(recv1, send1.at[peer], s1.at[peer], r1, peer, "seq").wait_recv()

    each(S - 1, wait1)
    tops = recv1[:, :, DH : DH + 1]
    sums = recv1[:, :, DH + DH // 2 : DH + DH // 2 + 1]
    high = jnp.max(tops, axis=0, keepdims=True)
    shrink = jnp.exp(tops - high)
    whole = jnp.sum(sums * shrink, axis=0)
    context = jnp.sum(recv1[:, :, :DH] * shrink, axis=0) / whole
    context = context.astype(BF16).astype(F32)
    own_cols = iota((pack, cols), 1) // DH == lax.rem(iota((pack, cols), 0), heads)
    tiled = jnp.where(own_cols, jnp.concatenate([context] * heads, axis=1), 0.0)

    def lift(pieces, columns):
        at = iota((8, columns), 0)
        out = jnp.zeros((8, columns), F32)
        for i, piece in enumerate(pieces):
            out = jnp.where(at == i, piece, out)
        return out

    tiled_row = iota((pack, cols), 0) // heads
    flat = lift(
        [
            jnp.sum(jnp.where(tiled_row == i, tiled, 0.0), axis=0, keepdims=True)
            for i in range(own)
        ],
        cols,
    ).astype(BF16)
    out_copy.wait()
    part = dot(flat, wout[...])
    send2[...] = part[:own]

    def copy2(peer):
        return pltpu.make_async_remote_copy(
            send2, recv2.at[mp], s2.at[peer], r2.at[mp],
            device_id={"mp": peer}, device_id_type=MESH,
        )

    each(M - 1, lambda o: copy2(lax.rem(mp + 1 + o, M)).start())
    recv2[mp] = send2[...]
    pick = (
        (iota((8, rows), 1) == me * own + iota((8, rows), 0)) & (iota((8, rows), 0) < own)
    ).astype(F32).astype(BF16)
    mine_x = dot(pick, x.astype(BF16))

    def wait2(o):
        peer = lax.rem(mp + 1 + o, M)
        came(recv2, send2, s2.at[peer], r2, peer, "mp").wait_recv()

    each(M - 1, wait2)
    attn = recv2[0]
    for j in range(1, M):
        attn = attn + recv2[j]
    middle = mine_x + lift([attn[i : i + 1] for i in range(own)], width)
    normed_mid = layer_norm(middle).astype(BF16)
    for j in range(M):
        mids[j] = middle[:own, j * cols : (j + 1) * cols]
    gate_copy.wait()
    gate = dot(normed_mid, wgu[0])
    up_copy.wait()
    up = dot(normed_mid, wgu[1])
    active = (gate / (1.0 + jnp.exp(-gate)) * up).astype(BF16)
    down_copy.wait()
    part = dot(active, wdown[...])
    for j in range(M):
        send3[j] = part[:own, j * cols : (j + 1) * cols]

    def copy3(peer):
        return pltpu.make_async_remote_copy(
            send3.at[peer], recv3.at[mp], s3.at[peer], r3.at[mp],
            device_id={"mp": peer}, device_id_type=MESH,
        )

    each(M - 1, lambda o: copy3(lax.rem(mp + 1 + o, M)).start())
    recv3[mp] = send3[mp]

    def wait3(o):
        peer = lax.rem(mp + 1 + o, M)
        came(recv3, send3.at[peer], s3.at[peer], r3, peer, "mp").wait_recv()

    each(M - 1, wait3)
    hidden = recv3[0]
    for j in range(1, M):
        hidden = hidden + recv3[j]
    send4[...] = (mids[mp] + hidden).astype(BF16).astype(F32)

    def copy4(peer):
        return pltpu.make_async_remote_copy(
            send4, recv4.at[me], s4.at[peer], r4.at[me],
            device_id={"seq": peer}, device_id_type=MESH,
        )

    each(S - 1, lambda o: copy4(lax.rem(me + 1 + o, S)).start())
    recv4[me] = send4[...]

    def wait4(o):
        peer = lax.rem(me + 1 + o, S)
        came(recv4, send4, s4.at[peer], r4, peer, "seq").wait_recv()

    each(S - 1, wait4)
    h_out[...] = recv4[...]

    each(S - 1, lambda o: copy1(lax.rem(me + 1 + o, S)).wait_send())
    each(M - 1, lambda o: copy2(lax.rem(mp + 1 + o, M)).wait_send())
    each(M - 1, lambda o: copy3(lax.rem(mp + 1 + o, M)).wait_send())
    each(S - 1, lambda o: copy4(lax.rem(me + 1 + o, S)).wait_send())


def per_device(S, M, inputs, w_qkv, w_out, w_gate_up, w_down, cache_keys, cache_values, lengths):
    batch, steps, width = inputs.shape
    rows = batch * steps
    cols = w_qkv.shape[2]
    heads = cols // DH
    own = rows // S
    pack = own * heads
    half = DH // 2
    inverse = BASE ** (-2.0 * jnp.arange(half, dtype=F32) / DH)
    positions = (lengths[:, None] + jnp.arange(steps, dtype=jnp.int32)[None, :]).reshape(rows)
    angles = positions.astype(F32)[:, None] * inverse
    cos, sin = jnp.cos(angles), jnp.sin(angles)
    table = jnp.stack(
        [jnp.concatenate([cos, cos], axis=1), jnp.concatenate([-sin, sin], axis=1)]
    )
    anywhere = pl.BlockSpec(memory_space=pl.ANY)
    vmem = pl.BlockSpec(memory_space=pltpu.VMEM)
    small = jax.ShapeDtypeStruct((rows, cols), F32)
    dma = pltpu.SemaphoreType.DMA
    queries, keys, values, hidden = pl.pallas_call(
        functools.partial(kernel, S, M),
        out_shape=[small, small, small, jax.ShapeDtypeStruct((S, own, cols), F32)],
        in_specs=[pl.BlockSpec(memory_space=pltpu.SMEM)] + [anywhere] * 8,
        out_specs=[vmem] * 4,
        scratch_shapes=[
            pltpu.VMEM(inputs.shape, BF16),
            pltpu.VMEM(table.shape, F32),
            pltpu.VMEM(w_qkv.shape, BF16),
            pltpu.VMEM(w_out.shape, BF16),
            pltpu.VMEM(w_gate_up.shape, BF16),
            pltpu.VMEM(w_down.shape, BF16),
            pltpu.VMEM(cache_keys.shape, BF16),
            pltpu.VMEM(cache_values.shape, BF16),
            pltpu.VMEM((rows, width), F32),
            pltpu.VMEM((S, pack, 2 * DH), F32),
            pltpu.VMEM((S, pack, 2 * DH), F32),
            pltpu.VMEM((own, width), F32),
            pltpu.VMEM((M, own, width), F32),
            pltpu.VMEM((M, own, cols), F32),
            pltpu.VMEM((M, own, cols), F32),
            pltpu.VMEM((M, own, cols), F32),
            pltpu.VMEM((own, cols), F32),
            pltpu.VMEM((S, own, cols), F32),
            dma((2,)),
            dma((3, QKV_CUTS)),
            dma((4,)),
            dma((2,)),
            dma((S,)),
            dma((S,)),
            dma((M,)),
            dma((M,)),
            dma((M,)),
            dma((M,)),
            dma((S,)),
            dma((S,)),
        ],
        compiler_params=pltpu.CompilerParams(
            collective_id=0, has_side_effects=True, vmem_limit_bytes=60 * 1024 * 1024
        ),
        name="layer",
    )(lengths, inputs, table, w_qkv, w_out, w_gate_up, w_down, cache_keys, cache_values)
    shape = (batch, steps, cols)
    return tuple(a.reshape(shape).astype(BF16) for a in (hidden, queries, keys, values))


def solution(mesh):
    cut = P(None, None, "mp")
    cache = P(None, "seq", "mp")
    return jax.shard_map(
        functools.partial(per_device, mesh.shape["seq"], mesh.shape["mp"]),
        mesh=mesh,
        in_specs=(P(), cut, P("mp", None), cut, P("mp", None), cache, cache, P()),
        out_specs=(cut,) * 4,
        check_vma=False,
    )
```

```python
import functools
import math

import jax
import jax.numpy as jnp
from jax import lax
from jax.experimental import pallas as pl
from jax.experimental.pallas import tpu as pltpu
from jax.sharding import PartitionSpec as P

DH = 128
NEG = -1e30
EPS = 1e-05
BASE = 10000.0
MESH = pl.DeviceIdType.MESH
F32 = jnp.float32
BF16 = jnp.bfloat16
QKV_CUTS = 4


def each(count, body):
    if count <= 8:
        for i in range(count):
            body(i)
    else:
        lax.fori_loop(0, count, lambda i, c: (body(i), c)[1], 0)


def iota(shape, axis):
    return lax.broadcasted_iota(jnp.int32, shape, axis)


def layer_norm(values):
    average = jnp.mean(values, axis=-1, keepdims=True)
    centred = values - average
    variance = jnp.mean(centred * centred, axis=-1, keepdims=True)
    return centred * lax.rsqrt(variance + EPS)


def dot(a, b):
    return jnp.dot(a, b, preferred_element_type=F32)


def kernel(
    S, M,
    len_hbm, x_hbm, wqkv_hbm, wout_hbm, wgu_hbm, wdown_hbm, ck_hbm, cv_hbm,
    q_out, k_out, v_out, h_out,
    len_ref, x_in, qf, kf, vf, hf, wides, wqkv, wout, wgu, wdown, ck, cv,
    xf, send1, recv1, send2, recv2, send3, recv3, mids, send4, recv4,
    xsem, qsem, wsem, csem, s1, r1, s2, r2, s3, r3, s4, r4,
):
    batch, steps, width = x_in.shape
    rows = batch * steps
    block = ck.shape[1]
    cols = wqkv.shape[2]
    heads = cols // DH
    own = rows // S
    pack = own * heads
    me = lax.axis_index("seq")
    mp = lax.axis_index("mp")

    x_copy = pltpu.make_async_copy(x_hbm, x_in, xsem.at[0])
    len_copy = pltpu.make_async_copy(len_hbm, len_ref, xsem.at[1])
    x_copy.start()
    len_copy.start()
    cut = width // QKV_CUTS
    q_copies = [
        [
            pltpu.make_async_copy(
                wqkv_hbm.at[j, pl.ds(c * cut, cut)], wqkv.at[j, pl.ds(c * cut, cut)], qsem.at[j, c]
            )
            for c in range(QKV_CUTS)
        ]
        for j in range(3)
    ]
    for c in range(QKV_CUTS):
        q_copies[0][c].start()
    ck_copy = pltpu.make_async_copy(ck_hbm, ck, csem.at[0])
    cv_copy = pltpu.make_async_copy(cv_hbm, cv, csem.at[1])
    ck_copy.start()
    cv_copy.start()
    out_copy = pltpu.make_async_copy(wout_hbm, wout, wsem.at[0])
    gate_copy = pltpu.make_async_copy(wgu_hbm.at[0], wgu.at[0], wsem.at[1])
    up_copy = pltpu.make_async_copy(wgu_hbm.at[1], wgu.at[1], wsem.at[2])
    down_copy = pltpu.make_async_copy(wdown_hbm, wdown, wsem.at[3])

    barrier = pltpu.get_barrier_semaphore()

    def greet_seq(o):
        pl.semaphore_signal(
            barrier, inc=1, device_id={"seq": lax.rem(me + 1 + o, S)}, device_id_type=MESH
        )

    def greet_mp(o):
        pl.semaphore_signal(
            barrier, inc=1, device_id={"mp": lax.rem(mp + 1 + o, M)}, device_id_type=MESH
        )

    each(S - 1, greet_seq)
    each(M - 1, greet_mp)

    x_copy.wait()
    for r in range(batch):
        xf[r * steps : (r + 1) * steps, :] = x_in[r].astype(F32)
    x = xf[...]
    normed = layer_norm(x).astype(BF16)

    def project(j):
        total = None
        for c in range(QKV_CUTS):
            q_copies[j][c].wait()
            if j == 0:
                q_copies[1][c].start()
            if j == 1:
                q_copies[2][c].start()
            term = dot(normed[:, c * cut : (c + 1) * cut], wqkv[j, c * cut : (c + 1) * cut, :])
            total = term if total is None else total + term
        return total

    len_copy.wait()
    token = iota((rows, DH), 0)
    position = lax.rem(token, steps)
    for r in range(batch):
        position = position + jnp.where(token // steps == r, len_ref[r], 0)
    lane = iota((rows, DH), 1)
    fold = lax.rem(lane, DH // 2).astype(F32)
    angle = position.astype(F32) * jnp.exp(fold * (-2.0 * math.log(BASE) / DH))
    cos = jnp.cos(angle)
    sin = jnp.sin(angle)
    sin = jnp.where(lane < DH // 2, -sin, sin)

    def rope(values, ref):
        for h in range(heads):
            v = values[:, h * DH : (h + 1) * DH]
            turned = pltpu.roll(v, DH // 2, 1)
            ref[:, h * DH : (h + 1) * DH] = (v * cos + turned * sin).astype(BF16).astype(F32)

    def emit(ref, out):
        for r in range(batch):
            out[r] = ref[r * steps : (r + 1) * steps, :].astype(BF16)

    rope(project(0), qf)

    full = rows * heads
    spread = (iota((full, rows), 0) // heads == iota((full, rows), 1)).astype(F32).astype(BF16)
    wide = dot(spread, qf[...].astype(BF16))
    own_cols = iota((full, cols), 1) // DH == lax.rem(iota((full, cols), 0), heads)
    wide = jnp.where(own_cols, wide, 0.0)
    wides[...] = wide.reshape(S, pack, cols)
    wide = wide.astype(BF16)

    nt = (((1,), (1,)), ((), ()))
    scale = DH ** -0.5
    group = steps * heads
    ck_copy.wait()
    parts = []
    for r in range(batch):
        raw = lax.dot_general(
            wide[r * group : (r + 1) * group], ck[r], nt, preferred_element_type=F32
        )
        place = iota((group, block), 1) + me * block
        parts.append(jnp.where(place < len_ref[r], raw * scale, NEG))
    scores = jnp.concatenate(parts, axis=0)
    top = jnp.max(scores, axis=1, keepdims=True)
    weights = jnp.where(scores > 0.5 * NEG, jnp.exp(scores - top), 0.0)
    total = jnp.sum(weights, axis=1, keepdims=True)
    cv_copy.wait()
    weights = weights.astype(BF16)
    summed = jnp.concatenate(
        [dot(weights[r * group : (r + 1) * group], cv[r]) for r in range(batch)], axis=0
    )

    def by_head(wide_rows):
        head_of = lax.rem(iota((wide_rows.shape[0], DH), 0), heads)
        out = jnp.zeros((wide_rows.shape[0], DH), F32)
        for h in range(heads):
            out = out + jnp.where(head_of == h, wide_rows[:, h * DH : (h + 1) * DH], 0.0)
        return out

    stats = jnp.where(iota((full, DH), 1) < DH // 2, top, total)
    send1[:, :, :DH] = by_head(summed).reshape(S, pack, DH)
    send1[:, :, DH:] = stats.reshape(S, pack, DH)

    pl.semaphore_wait(barrier, S + M - 2)

    def copy1(peer):
        return pltpu.make_async_remote_copy(
            send1.at[peer], recv1.at[me], s1.at[peer], r1.at[me],
            device_id={"seq": peer}, device_id_type=MESH,
        )

    def came(buf, src, send_sem, recv_sem, slot, axis):
        return pltpu.make_async_remote_copy(
            src, buf.at[slot], send_sem, recv_sem.at[slot],
            device_id={axis: slot}, device_id_type=MESH,
        )

    each(S - 1, lambda o: copy1(lax.rem(me + 1 + o, S)).start())
    recv1[me] = send1[me]

    keys = project(1)
    out_copy.start()
    gate_copy.start()
    rope(keys, kf)
    values = project(2)
    up_copy.start()
    down_copy.start()
    vf[...] = values.astype(BF16).astype(F32)
    fresh = (
        lax.dot_general(
            wides[me].astype(BF16), kf[...].astype(BF16), nt, preferred_element_type=F32
        )
        * scale
    )
    row = me * pack + iota((pack, rows), 0)
    col = iota((pack, rows), 1)
    live = (row // group == col // steps) & (lax.rem(col, steps) <= lax.rem(row // heads, steps))
    fresh = jnp.where(live, fresh, NEG)
    fresh_top = jnp.max(fresh, axis=1, keepdims=True)
    fresh_w = jnp.where(live, jnp.exp(fresh - fresh_top), 0.0)
    fresh_total = jnp.sum(fresh_w, axis=1, keepdims=True)
    fresh_sum = by_head(dot(fresh_w.astype(BF16), vf[...].astype(BF16)))
    emit(qf, q_out)
    emit(kf, k_out)
    emit(vf, v_out)

    def wait1(o):
        peer = lax.rem(me + 1 + o, S)
        came(recv1, send1.at[peer], s1.at[peer], r1, peer, "seq").wait_recv()

    each(S - 1, wait1)
    tops = recv1[:, :, DH : DH + 1]
    sums = recv1[:, :, DH + DH // 2 : DH + DH // 2 + 1]
    high = jnp.maximum(jnp.max(tops, axis=0), fresh_top)
    shrink = jnp.exp(tops - high[None])
    fresh_shrink = jnp.exp(fresh_top - high)
    whole = jnp.sum(sums * shrink, axis=0) + fresh_total * fresh_shrink
    context = jnp.sum(recv1[:, :, :DH] * shrink, axis=0) + fresh_sum * fresh_shrink
    context = context / whole
    context = context.astype(BF16).astype(F32)
    own_cols = iota((pack, cols), 1) // DH == lax.rem(iota((pack, cols), 0), heads)
    tiled = jnp.where(own_cols, jnp.concatenate([context] * heads, axis=1), 0.0)

    def lift(pieces, columns):
        at = iota((8, columns), 0)
        out = jnp.zeros((8, columns), F32)
        for i, piece in enumerate(pieces):
            out = jnp.where(at == i, piece, out)
        return out

    tiled_row = iota((pack, cols), 0) // heads
    flat = lift(
        [
            jnp.sum(jnp.where(tiled_row == i, tiled, 0.0), axis=0, keepdims=True)
            for i in range(own)
        ],
        cols,
    ).astype(BF16)
    out_copy.wait()
    part = dot(flat, wout[...])
    send2[...] = part[:own]

    def copy2(peer):
        return pltpu.make_async_remote_copy(
            send2, recv2.at[mp], s2.at[peer], r2.at[mp],
            device_id={"mp": peer}, device_id_type=MESH,
        )

    each(M - 1, lambda o: copy2(lax.rem(mp + 1 + o, M)).start())
    recv2[mp] = send2[...]
    pick = (
        (iota((8, rows), 1) == me * own + iota((8, rows), 0)) & (iota((8, rows), 0) < own)
    ).astype(F32).astype(BF16)
    mine_x = dot(pick, x.astype(BF16))

    def wait2(o):
        peer = lax.rem(mp + 1 + o, M)
        came(recv2, send2, s2.at[peer], r2, peer, "mp").wait_recv()

    each(M - 1, wait2)
    attn = recv2[0]
    for j in range(1, M):
        attn = attn + recv2[j]
    middle = mine_x + lift([attn[i : i + 1] for i in range(own)], width)
    normed_mid = layer_norm(middle).astype(BF16)
    for j in range(M):
        mids[j] = middle[:own, j * cols : (j + 1) * cols]
    gate_copy.wait()
    gate = dot(normed_mid, wgu[0])
    up_copy.wait()
    up = dot(normed_mid, wgu[1])
    active = (gate / (1.0 + jnp.exp(-gate)) * up).astype(BF16)
    down_copy.wait()
    part = dot(active, wdown[...])
    for j in range(M):
        send3[j] = part[:own, j * cols : (j + 1) * cols]

    def copy3(peer):
        return pltpu.make_async_remote_copy(
            send3.at[peer], recv3.at[mp], s3.at[peer], r3.at[mp],
            device_id={"mp": peer}, device_id_type=MESH,
        )

    each(M - 1, lambda o: copy3(lax.rem(mp + 1 + o, M)).start())
    recv3[mp] = send3[mp]

    def wait3(o):
        peer = lax.rem(mp + 1 + o, M)
        came(recv3, send3.at[peer], s3.at[peer], r3, peer, "mp").wait_recv()

    each(M - 1, wait3)
    hidden = recv3[0]
    for j in range(1, M):
        hidden = hidden + recv3[j]
    send4[...] = (mids[mp] + hidden).astype(BF16).astype(F32)

    def copy4(peer):
        return pltpu.make_async_remote_copy(
            send4, recv4.at[me], s4.at[peer], r4.at[me],
            device_id={"seq": peer}, device_id_type=MESH,
        )

    each(S - 1, lambda o: copy4(lax.rem(me + 1 + o, S)).start())
    recv4[me] = send4[...]

    def wait4(o):
        peer = lax.rem(me + 1 + o, S)
        came(recv4, send4, s4.at[peer], r4, peer, "seq").wait_recv()

    each(S - 1, wait4)
    for i in range(S):
        hf[i * own : (i + 1) * own, :] = recv4[i]
    emit(hf, h_out)

    each(S - 1, lambda o: copy1(lax.rem(me + 1 + o, S)).wait_send())
    each(M - 1, lambda o: copy2(lax.rem(mp + 1 + o, M)).wait_send())
    each(M - 1, lambda o: copy3(lax.rem(mp + 1 + o, M)).wait_send())
    each(S - 1, lambda o: copy4(lax.rem(me + 1 + o, S)).wait_send())


def deliver(*refs):
    sems = refs[-1]
    count = len(refs) // 2
    copies = [
        pltpu.make_async_copy(refs[i], refs[count + i], sems.at[i]) for i in range(count)
    ]
    for copy in copies:
        copy.start()
    for copy in copies:
        copy.wait()


def per_device(S, M, inputs, w_qkv, w_out, w_gate_up, w_down, cache_keys, cache_values, lengths):
    batch, steps, width = inputs.shape
    rows = batch * steps
    cols = w_qkv.shape[2]
    heads = cols // DH
    own = rows // S
    pack = own * heads
    anywhere = pl.BlockSpec(memory_space=pl.ANY)
    vmem = pl.BlockSpec(memory_space=pltpu.VMEM)
    shape = (batch, steps, cols)
    small = pltpu.VMEM((rows, cols), F32)
    dma = pltpu.SemaphoreType.DMA
    results = pl.pallas_call(
        functools.partial(kernel, S, M),
        out_shape=[pltpu.VMEM(shape, BF16)] * 4,
        in_specs=[anywhere] * 8,
        out_specs=[vmem] * 4,
        scratch_shapes=[
            pltpu.SMEM(lengths.shape, jnp.int32),
            pltpu.VMEM(inputs.shape, BF16),
            small,
            small,
            small,
            small,
            pltpu.VMEM((S, pack, cols), F32),
            pltpu.VMEM(w_qkv.shape, BF16),
            pltpu.VMEM(w_out.shape, BF16),
            pltpu.VMEM(w_gate_up.shape, BF16),
            pltpu.VMEM(w_down.shape, BF16),
            pltpu.VMEM(cache_keys.shape, BF16),
            pltpu.VMEM(cache_values.shape, BF16),
            pltpu.VMEM((rows, width), F32),
            pltpu.VMEM((S, pack, 2 * DH), F32),
            pltpu.VMEM((S, pack, 2 * DH), F32),
            pltpu.VMEM((own, width), F32),
            pltpu.VMEM((M, own, width), F32),
            pltpu.VMEM((M, own, cols), F32),
            pltpu.VMEM((M, own, cols), F32),
            pltpu.VMEM((M, own, cols), F32),
            pltpu.VMEM((own, cols), F32),
            pltpu.VMEM((S, own, cols), F32),
            dma((2,)),
            dma((3, QKV_CUTS)),
            dma((4,)),
            dma((2,)),
            dma((S,)),
            dma((S,)),
            dma((M,)),
            dma((M,)),
            dma((M,)),
            dma((M,)),
            dma((S,)),
            dma((S,)),
        ],
        compiler_params=pltpu.CompilerParams(
            collective_id=0, has_side_effects=True, vmem_limit_bytes=60 * 1024 * 1024
        ),
        name="layer",
    )(lengths, inputs, w_qkv, w_out, w_gate_up, w_down, cache_keys, cache_values)
    queries, keys, values, hidden = results
    return tuple(
        pl.pallas_call(
            deliver,
            out_shape=[jax.ShapeDtypeStruct(shape, BF16)] * 4,
            in_specs=[vmem] * 4,
            out_specs=[anywhere] * 4,
            scratch_shapes=[dma((4,))],
            name="deliver",
        )(hidden, queries, keys, values)
    )


def solution(mesh):
    cut = P(None, None, "mp")
    cache = P(None, "seq", "mp")
    return jax.shard_map(
        functools.partial(per_device, mesh.shape["seq"], mesh.shape["mp"]),
        mesh=mesh,
        in_specs=(P(), cut, P("mp", None), cut, P("mp", None), cache, cache, P()),
        out_specs=(cut,) * 4,
        check_vma=False,
    )
```

```python
import functools
import math

import jax
import jax.numpy as jnp
from jax import lax
from jax.experimental import pallas as pl
from jax.experimental.pallas import tpu as pltpu
from jax.sharding import PartitionSpec as P

DH = 128
NEG = -1e30
EPS = 1e-05
BASE = 10000.0
MESH = pl.DeviceIdType.MESH
F32 = jnp.float32
BF16 = jnp.bfloat16
QKV_CUTS = 4
HALVES = 2


def each(count, body):
    if count <= 8:
        for i in range(count):
            body(i)
    else:
        lax.fori_loop(0, count, lambda i, c: (body(i), c)[1], 0)


def iota(shape, axis):
    return lax.broadcasted_iota(jnp.int32, shape, axis)


def layer_norm(values):
    average = jnp.mean(values, axis=-1, keepdims=True)
    centred = values - average
    variance = jnp.mean(centred * centred, axis=-1, keepdims=True)
    return centred * lax.rsqrt(variance + EPS)


def dot(a, b):
    return jnp.dot(a, b, preferred_element_type=F32)


def kernel(
    S, M,
    len_hbm, x_hbm, wqkv_hbm, wout_hbm, wgu_hbm, wdown_hbm, ck_hbm, cv_hbm,
    q_out, k_out, v_out, h_out,
    len_ref, x_in, qf, kf, vf, hf, wides, wqkv, wout, wgu, wdown, ck, cv,
    xf, send1, recv1, send2, recv2, send3, recv3, mids, send4, recv4,
    xsem, qsem, wsem, csem, s1, r1, s2, r2, s3, r3, s4, r4,
):
    batch, steps, width = x_in.shape
    rows = batch * steps
    block = ck.shape[1]
    cols = wqkv.shape[2]
    heads = cols // DH
    own = rows // S
    pack = own * heads
    me = lax.axis_index("seq")
    mp = lax.axis_index("mp")

    x_copy = pltpu.make_async_copy(x_hbm, x_in, xsem.at[0])
    len_copy = pltpu.make_async_copy(len_hbm, len_ref, xsem.at[1])
    x_copy.start()
    len_copy.start()
    cut = width // QKV_CUTS
    q_copies = [
        [
            pltpu.make_async_copy(
                wqkv_hbm.at[j, pl.ds(c * cut, cut)], wqkv.at[j, pl.ds(c * cut, cut)], qsem.at[j, c]
            )
            for c in range(QKV_CUTS)
        ]
        for j in range(3)
    ]
    for c in range(QKV_CUTS):
        q_copies[0][c].start()
    ck_copy = pltpu.make_async_copy(ck_hbm, ck, csem.at[0])
    cv_copy = pltpu.make_async_copy(cv_hbm, cv, csem.at[1])
    ck_copy.start()
    cv_copy.start()
    out_copy = pltpu.make_async_copy(wout_hbm, wout, wsem.at[0])
    gate_copy = pltpu.make_async_copy(wgu_hbm.at[0], wgu.at[0], wsem.at[1])
    up_copy = pltpu.make_async_copy(wgu_hbm.at[1], wgu.at[1], wsem.at[2])
    down_copy = pltpu.make_async_copy(wdown_hbm, wdown, wsem.at[3])

    barrier = pltpu.get_barrier_semaphore()

    def greet_seq(o):
        pl.semaphore_signal(
            barrier, inc=1, device_id={"seq": lax.rem(me + 1 + o, S)}, device_id_type=MESH
        )

    def greet_mp(o):
        pl.semaphore_signal(
            barrier, inc=1, device_id={"mp": lax.rem(mp + 1 + o, M)}, device_id_type=MESH
        )

    each(S - 1, greet_seq)
    each(M - 1, greet_mp)

    x_copy.wait()
    for r in range(batch):
        xf[r * steps : (r + 1) * steps, :] = x_in[r].astype(F32)
    x = xf[...]
    normed = layer_norm(x).astype(BF16)

    def project(j):
        total = None
        for c in range(QKV_CUTS):
            q_copies[j][c].wait()
            if j == 0:
                q_copies[1][c].start()
                q_copies[2][c].start()
            term = dot(normed[:, c * cut : (c + 1) * cut], wqkv[j, c * cut : (c + 1) * cut, :])
            total = term if total is None else total + term
        return total

    len_copy.wait()
    token = iota((rows, DH), 0)
    position = lax.rem(token, steps)
    for r in range(batch):
        position = position + jnp.where(token // steps == r, len_ref[r], 0)
    lane = iota((rows, DH), 1)
    fold = lax.rem(lane, DH // 2).astype(F32)
    angle = position.astype(F32) * jnp.exp(fold * (-2.0 * math.log(BASE) / DH))
    cos = jnp.cos(angle)
    sin = jnp.sin(angle)
    sin = jnp.where(lane < DH // 2, -sin, sin)

    def rope(values, ref):
        for h in range(heads):
            v = values[:, h * DH : (h + 1) * DH]
            turned = pltpu.roll(v, DH // 2, 1)
            ref[:, h * DH : (h + 1) * DH] = (v * cos + turned * sin).astype(BF16).astype(F32)

    def emit(ref, out):
        for r in range(batch):
            out[r] = ref[r * steps : (r + 1) * steps, :].astype(BF16)

    rope(project(0), qf)

    full = rows * heads
    spread = (iota((full, rows), 0) // heads == iota((full, rows), 1)).astype(F32).astype(BF16)
    wide = dot(spread, qf[...].astype(BF16))
    own_cols = iota((full, cols), 1) // DH == lax.rem(iota((full, cols), 0), heads)
    wide = jnp.where(own_cols, wide, 0.0)
    wides[...] = wide.reshape(S, pack, cols)
    wide = wide.astype(BF16)

    nt = (((1,), (1,)), ((), ()))
    scale = DH ** -0.5
    group = steps * heads
    ck_copy.wait()
    out_copy.start()
    parts = []
    for r in range(batch):
        raw = lax.dot_general(
            wide[r * group : (r + 1) * group], ck[r], nt, preferred_element_type=F32
        )
        place = iota((group, block), 1) + me * block
        parts.append(jnp.where(place < len_ref[r], raw * scale, NEG))
    scores = jnp.concatenate(parts, axis=0)
    top = jnp.max(scores, axis=1, keepdims=True)
    weights = jnp.where(scores > 0.5 * NEG, jnp.exp(scores - top), 0.0)
    total = jnp.sum(weights, axis=1, keepdims=True)
    cv_copy.wait()
    gate_copy.start()
    weights = weights.astype(BF16)
    summed = jnp.concatenate(
        [dot(weights[r * group : (r + 1) * group], cv[r]) for r in range(batch)], axis=0
    )

    def by_head(wide_rows):
        head_of = lax.rem(iota((wide_rows.shape[0], DH), 0), heads)
        out = jnp.zeros((wide_rows.shape[0], DH), F32)
        for h in range(heads):
            out = out + jnp.where(head_of == h, wide_rows[:, h * DH : (h + 1) * DH], 0.0)
        return out

    stats = jnp.where(iota((full, DH), 1) < DH // 2, top, total)
    send1[:, :, :DH] = by_head(summed).reshape(S, pack, DH)
    send1[:, :, DH:] = stats.reshape(S, pack, DH)

    pl.semaphore_wait(barrier, S + M - 2)

    def copy1(peer):
        return pltpu.make_async_remote_copy(
            send1.at[peer], recv1.at[me], s1.at[peer], r1.at[me],
            device_id={"seq": peer}, device_id_type=MESH,
        )

    def came(buf, src, send_sem, recv_sem, slot, axis):
        return pltpu.make_async_remote_copy(
            src, buf.at[slot], send_sem, recv_sem.at[slot],
            device_id={axis: slot}, device_id_type=MESH,
        )

    each(S - 1, lambda o: copy1(lax.rem(me + 1 + o, S)).start())
    recv1[me] = send1[me]

    up_copy.start()
    keys = project(1)
    down_copy.start()
    rope(keys, kf)
    values = project(2)
    vf[...] = values.astype(BF16).astype(F32)
    fresh = (
        lax.dot_general(
            wides[me].astype(BF16), kf[...].astype(BF16), nt, preferred_element_type=F32
        )
        * scale
    )
    row = me * pack + iota((pack, rows), 0)
    col = iota((pack, rows), 1)
    live = (row // group == col // steps) & (lax.rem(col, steps) <= lax.rem(row // heads, steps))
    fresh = jnp.where(live, fresh, NEG)
    fresh_top = jnp.max(fresh, axis=1, keepdims=True)
    fresh_w = jnp.where(live, jnp.exp(fresh - fresh_top), 0.0)
    fresh_total = jnp.sum(fresh_w, axis=1, keepdims=True)
    fresh_sum = by_head(dot(fresh_w.astype(BF16), vf[...].astype(BF16)))
    emit(qf, q_out)
    emit(kf, k_out)
    emit(vf, v_out)

    def wait1(o):
        peer = lax.rem(me + 1 + o, S)
        came(recv1, send1.at[peer], s1.at[peer], r1, peer, "seq").wait_recv()

    each(S - 1, wait1)
    tops = recv1[:, :, DH : DH + 1]
    sums = recv1[:, :, DH + DH // 2 : DH + DH // 2 + 1]
    high = jnp.maximum(jnp.max(tops, axis=0), fresh_top)
    shrink = jnp.exp(tops - high[None])
    fresh_shrink = jnp.exp(fresh_top - high)
    whole = jnp.sum(sums * shrink, axis=0) + fresh_total * fresh_shrink
    context = jnp.sum(recv1[:, :, :DH] * shrink, axis=0) + fresh_sum * fresh_shrink
    context = context / whole
    context = context.astype(BF16).astype(F32)
    own_cols = iota((pack, cols), 1) // DH == lax.rem(iota((pack, cols), 0), heads)
    tiled = jnp.where(own_cols, jnp.concatenate([context] * heads, axis=1), 0.0)

    def lift(pieces, columns):
        at = iota((8, columns), 0)
        out = jnp.zeros((8, columns), F32)
        for i, piece in enumerate(pieces):
            out = jnp.where(at == i, piece, out)
        return out

    tiled_row = iota((pack, cols), 0) // heads
    flat = lift(
        [
            jnp.sum(jnp.where(tiled_row == i, tiled, 0.0), axis=0, keepdims=True)
            for i in range(own)
        ],
        cols,
    ).astype(BF16)
    out_copy.wait()
    half = width // HALVES

    def copy2(p, peer):
        return pltpu.make_async_remote_copy(
            send2.at[p], recv2.at[p, mp], s2.at[p, peer], r2.at[p, mp],
            device_id={"mp": peer}, device_id_type=MESH,
        )

    others = sorted(range(1, M), key=lambda o: abs(o - M // 2))
    for p in range(HALVES):
        send2[p] = dot(flat, wout[:, p * half : (p + 1) * half])[:own]
        for o in others:
            copy2(p, lax.rem(mp + o, M)).start()
        recv2[p, mp] = send2[p]
    pick = (
        (iota((8, rows), 1) == me * own + iota((8, rows), 0)) & (iota((8, rows), 0) < own)
    ).astype(F32).astype(BF16)
    mine_x = dot(pick, x.astype(BF16))

    def landed2(p, peer):
        return pltpu.make_async_remote_copy(
            send2.at[p], recv2.at[p, peer], s2.at[p, peer], r2.at[p, peer],
            device_id={"mp": peer}, device_id_type=MESH,
        )

    lifted = []
    for p in range(HALVES):
        for o in others:
            landed2(p, lax.rem(mp + o, M)).wait_recv()
        attn = recv2[p, 0]
        for j in range(1, M):
            attn = attn + recv2[p, j]
        lifted.append(lift([attn[i : i + 1] for i in range(own)], half))
    middle = mine_x + jnp.concatenate(lifted, axis=1)
    normed_mid = layer_norm(middle).astype(BF16)
    for j in range(M):
        mids[j] = middle[:own, j * cols : (j + 1) * cols]
    gate_copy.wait()
    gate = dot(normed_mid, wgu[0])
    up_copy.wait()
    up = dot(normed_mid, wgu[1])
    active = (gate / (1.0 + jnp.exp(-gate)) * up).astype(BF16)
    down_copy.wait()

    def copy3(peer):
        return pltpu.make_async_remote_copy(
            send3.at[peer], recv3.at[mp], s3.at[peer], r3.at[mp],
            device_id={"mp": peer}, device_id_type=MESH,
        )

    def down_block(j):
        return dot(active, wdown[:, pl.ds(pl.multiple_of(j * cols, cols), cols)])[:own]

    for o in others:
        peer = lax.rem(mp + o, M)
        send3[peer] = down_block(peer)
        copy3(peer).start()
    recv3[mp] = down_block(mp)

    def wait3(o):
        peer = lax.rem(mp + 1 + o, M)
        came(recv3, send3.at[peer], s3.at[peer], r3, peer, "mp").wait_recv()

    each(M - 1, wait3)
    hidden = recv3[0]
    for j in range(1, M):
        hidden = hidden + recv3[j]
    send4[...] = (mids[mp] + hidden).astype(BF16).astype(F32)

    def copy4(peer):
        return pltpu.make_async_remote_copy(
            send4, recv4.at[me], s4.at[peer], r4.at[me],
            device_id={"seq": peer}, device_id_type=MESH,
        )

    each(S - 1, lambda o: copy4(lax.rem(me + 1 + o, S)).start())
    recv4[me] = send4[...]

    def wait4(o):
        peer = lax.rem(me + 1 + o, S)
        came(recv4, send4, s4.at[peer], r4, peer, "seq").wait_recv()

    each(S - 1, wait4)
    for i in range(S):
        hf[i * own : (i + 1) * own, :] = recv4[i]
    emit(hf, h_out)

    each(S - 1, lambda o: copy1(lax.rem(me + 1 + o, S)).wait_send())
    for p in range(HALVES):
        for o in others:
            copy2(p, lax.rem(mp + o, M)).wait_send()
    each(M - 1, lambda o: copy3(lax.rem(mp + 1 + o, M)).wait_send())
    each(S - 1, lambda o: copy4(lax.rem(me + 1 + o, S)).wait_send())


def deliver(*refs):
    sems = refs[-1]
    count = len(refs) // 2
    copies = [
        pltpu.make_async_copy(refs[i], refs[count + i], sems.at[i]) for i in range(count)
    ]
    for copy in copies:
        copy.start()
    for copy in copies:
        copy.wait()


def per_device(S, M, inputs, w_qkv, w_out, w_gate_up, w_down, cache_keys, cache_values, lengths):
    batch, steps, width = inputs.shape
    rows = batch * steps
    cols = w_qkv.shape[2]
    heads = cols // DH
    own = rows // S
    pack = own * heads
    anywhere = pl.BlockSpec(memory_space=pl.ANY)
    vmem = pl.BlockSpec(memory_space=pltpu.VMEM)
    shape = (batch, steps, cols)
    small = pltpu.VMEM((rows, cols), F32)
    dma = pltpu.SemaphoreType.DMA
    results = pl.pallas_call(
        functools.partial(kernel, S, M),
        out_shape=[pltpu.VMEM(shape, BF16)] * 4,
        in_specs=[anywhere] * 8,
        out_specs=[vmem] * 4,
        scratch_shapes=[
            pltpu.SMEM(lengths.shape, jnp.int32),
            pltpu.VMEM(inputs.shape, BF16),
            small,
            small,
            small,
            small,
            pltpu.VMEM((S, pack, cols), F32),
            pltpu.VMEM(w_qkv.shape, BF16),
            pltpu.VMEM(w_out.shape, BF16),
            pltpu.VMEM(w_gate_up.shape, BF16),
            pltpu.VMEM(w_down.shape, BF16),
            pltpu.VMEM(cache_keys.shape, BF16),
            pltpu.VMEM(cache_values.shape, BF16),
            pltpu.VMEM((rows, width), F32),
            pltpu.VMEM((S, pack, 2 * DH), F32),
            pltpu.VMEM((S, pack, 2 * DH), F32),
            pltpu.VMEM((HALVES, own, width // HALVES), F32),
            pltpu.VMEM((HALVES, M, own, width // HALVES), F32),
            pltpu.VMEM((M, own, cols), F32),
            pltpu.VMEM((M, own, cols), F32),
            pltpu.VMEM((M, own, cols), F32),
            pltpu.VMEM((own, cols), F32),
            pltpu.VMEM((S, own, cols), F32),
            dma((2,)),
            dma((3, QKV_CUTS)),
            dma((4,)),
            dma((2,)),
            dma((S,)),
            dma((S,)),
            dma((HALVES, M)),
            dma((HALVES, M)),
            dma((M,)),
            dma((M,)),
            dma((S,)),
            dma((S,)),
        ],
        compiler_params=pltpu.CompilerParams(
            collective_id=0, has_side_effects=True, vmem_limit_bytes=60 * 1024 * 1024
        ),
        name="layer",
    )(lengths, inputs, w_qkv, w_out, w_gate_up, w_down, cache_keys, cache_values)
    queries, keys, values, hidden = (
        pltpu.with_memory_space_constraint(a, pltpu.VMEM) for a in results
    )
    return tuple(
        pl.pallas_call(
            deliver,
            out_shape=[jax.ShapeDtypeStruct(shape, BF16)] * 4,
            in_specs=[vmem] * 4,
            out_specs=[anywhere] * 4,
            scratch_shapes=[dma((4,))],
            name="deliver",
        )(hidden, queries, keys, values)
    )


def solution(mesh):
    cut = P(None, None, "mp")
    cache = P(None, "seq", "mp")
    return jax.shard_map(
        functools.partial(per_device, mesh.shape["seq"], mesh.shape["mp"]),
        mesh=mesh,
        in_specs=(P(), cut, P("mp", None), cut, P("mp", None), cache, cache, P()),
        out_specs=(cut,) * 4,
        check_vma=False,
    )
```

```python
import functools
import math

import jax
import jax.numpy as jnp
from jax import lax
from jax.experimental import pallas as pl
from jax.experimental.pallas import tpu as pltpu
from jax.sharding import PartitionSpec as P

DH = 128
NEG = -1e30
EPS = 1e-05
BASE = 10000.0
MESH = pl.DeviceIdType.MESH
F32 = jnp.float32
BF16 = jnp.bfloat16
QKV_CUTS = 4
HALVES = 2


def each(count, body):
    if count <= 8:
        for i in range(count):
            body(i)
    else:
        lax.fori_loop(0, count, lambda i, c: (body(i), c)[1], 0)


def iota(shape, axis):
    return lax.broadcasted_iota(jnp.int32, shape, axis)


def layer_norm(values):
    average = jnp.mean(values, axis=-1, keepdims=True)
    centred = values - average
    variance = jnp.mean(centred * centred, axis=-1, keepdims=True)
    return centred * lax.rsqrt(variance + EPS)


def dot(a, b):
    return jnp.dot(a, b, preferred_element_type=F32)


def kernel(
    S, M,
    len_hbm, x_hbm, wqkv_hbm, wout_hbm, wgu_hbm, wdown_hbm, ck_hbm, cv_hbm,
    q_out, k_out, v_out, h_out,
    len_ref, x_in, qf, kf, vf, hf, wides, wqkv, wout, wgu, wdown, ck, cv,
    xf, send1, recv1, send2, recv2, send3, recv3, mids,
    xsem, qsem, wsem, csem, s1, r1, s2, r2, s3, r3,
):
    batch, steps, width = x_in.shape
    rows = batch * steps
    block = ck.shape[1]
    cols = wqkv.shape[2]
    heads = cols // DH
    own = rows // S
    pack = own * heads
    me = lax.axis_index("seq")
    mp = lax.axis_index("mp")

    x_copy = pltpu.make_async_copy(x_hbm, x_in, xsem.at[0])
    len_copy = pltpu.make_async_copy(len_hbm, len_ref, xsem.at[1])
    x_copy.start()
    len_copy.start()
    cut = width // QKV_CUTS
    q_copies = [
        [
            pltpu.make_async_copy(
                wqkv_hbm.at[j, pl.ds(c * cut, cut)], wqkv.at[j, pl.ds(c * cut, cut)], qsem.at[j, c]
            )
            for c in range(QKV_CUTS)
        ]
        for j in range(3)
    ]
    for c in range(QKV_CUTS):
        q_copies[0][c].start()
    ck_copy = pltpu.make_async_copy(ck_hbm, ck, csem.at[0])
    cv_copy = pltpu.make_async_copy(cv_hbm, cv, csem.at[1])
    ck_copy.start()
    cv_copy.start()
    out_copy = pltpu.make_async_copy(wout_hbm, wout, wsem.at[0])
    gate_copy = pltpu.make_async_copy(wgu_hbm.at[0], wgu.at[0], wsem.at[1])
    up_copy = pltpu.make_async_copy(wgu_hbm.at[1], wgu.at[1], wsem.at[2])
    down_copy = pltpu.make_async_copy(wdown_hbm, wdown, wsem.at[3])

    barrier = pltpu.get_barrier_semaphore()

    def greet(o):
        at = lax.rem(me * M + mp + 1 + o, S * M)
        pl.semaphore_signal(
            barrier, inc=1, device_id={"seq": at // M, "mp": lax.rem(at, M)}, device_id_type=MESH
        )

    if S * M <= 32:
        for o in range(S * M - 1):
            greet(o)
    else:
        each(S * M - 1, greet)

    x_copy.wait()
    for r in range(batch):
        xf[r * steps : (r + 1) * steps, :] = x_in[r].astype(F32)
    x = xf[...]
    normed = layer_norm(x).astype(BF16)

    def project(j):
        total = None
        for c in range(QKV_CUTS):
            q_copies[j][c].wait()
            if j == 0:
                q_copies[1][c].start()
                q_copies[2][c].start()
            term = dot(normed[:, c * cut : (c + 1) * cut], wqkv[j, c * cut : (c + 1) * cut, :])
            total = term if total is None else total + term
        return total

    len_copy.wait()
    token = iota((rows, DH), 0)
    position = lax.rem(token, steps)
    for r in range(batch):
        position = position + jnp.where(token // steps == r, len_ref[r], 0)
    lane = iota((rows, DH), 1)
    fold = lax.rem(lane, DH // 2).astype(F32)
    angle = position.astype(F32) * jnp.exp(fold * (-2.0 * math.log(BASE) / DH))
    cos = jnp.cos(angle)
    sin = jnp.sin(angle)
    sin = jnp.where(lane < DH // 2, -sin, sin)

    def rope(values, ref):
        for h in range(heads):
            v = values[:, h * DH : (h + 1) * DH]
            turned = pltpu.roll(v, DH // 2, 1)
            ref[:, h * DH : (h + 1) * DH] = (v * cos + turned * sin).astype(BF16).astype(F32)

    def emit(ref, out):
        for r in range(batch):
            out[r] = ref[r * steps : (r + 1) * steps, :].astype(BF16)

    rope(project(0), qf)

    full = rows * heads
    spread = (iota((full, rows), 0) // heads == iota((full, rows), 1)).astype(F32).astype(BF16)
    wide = dot(spread, qf[...].astype(BF16))
    own_cols = iota((full, cols), 1) // DH == lax.rem(iota((full, cols), 0), heads)
    wide = jnp.where(own_cols, wide, 0.0)
    wides[...] = wide.reshape(S, pack, cols)
    wide = wide.astype(BF16)

    nt = (((1,), (1,)), ((), ()))
    scale = DH ** -0.5
    group = steps * heads
    ck_copy.wait()
    out_copy.start()
    parts = []
    for r in range(batch):
        raw = lax.dot_general(
            wide[r * group : (r + 1) * group], ck[r], nt, preferred_element_type=F32
        )
        place = iota((group, block), 1) + me * block
        parts.append(jnp.where(place < len_ref[r], raw * scale, NEG))
    scores = jnp.concatenate(parts, axis=0)
    top = jnp.max(scores, axis=1, keepdims=True)
    weights = jnp.where(scores > 0.5 * NEG, jnp.exp(scores - top), 0.0)
    total = jnp.sum(weights, axis=1, keepdims=True)
    cv_copy.wait()
    gate_copy.start()
    weights = weights.astype(BF16)
    summed = jnp.concatenate(
        [dot(weights[r * group : (r + 1) * group], cv[r]) for r in range(batch)], axis=0
    )

    def by_head(wide_rows):
        head_of = lax.rem(iota((wide_rows.shape[0], DH), 0), heads)
        out = jnp.zeros((wide_rows.shape[0], DH), F32)
        for h in range(heads):
            out = out + jnp.where(head_of == h, wide_rows[:, h * DH : (h + 1) * DH], 0.0)
        return out

    stats = jnp.where(iota((full, DH), 1) < DH // 2, top, total)
    send1[:, :, :DH] = by_head(summed).reshape(S, pack, DH)
    send1[:, :, DH:] = stats.reshape(S, pack, DH)

    pl.semaphore_wait(barrier, S * M - 1)

    def copy1(peer):
        return pltpu.make_async_remote_copy(
            send1.at[peer], recv1.at[me], s1.at[peer], r1.at[me],
            device_id={"seq": peer}, device_id_type=MESH,
        )

    def came(buf, src, send_sem, recv_sem, slot, axis):
        return pltpu.make_async_remote_copy(
            src, buf.at[slot], send_sem, recv_sem.at[slot],
            device_id={axis: slot}, device_id_type=MESH,
        )

    each(S - 1, lambda o: copy1(lax.rem(me + 1 + o, S)).start())
    recv1[me] = send1[me]

    up_copy.start()
    keys = project(1)
    down_copy.start()
    rope(keys, kf)
    values = project(2)
    vf[...] = values.astype(BF16).astype(F32)
    fresh = (
        lax.dot_general(
            wides[me].astype(BF16), kf[...].astype(BF16), nt, preferred_element_type=F32
        )
        * scale
    )
    row = me * pack + iota((pack, rows), 0)
    col = iota((pack, rows), 1)
    live = (row // group == col // steps) & (lax.rem(col, steps) <= lax.rem(row // heads, steps))
    fresh = jnp.where(live, fresh, NEG)
    fresh_top = jnp.max(fresh, axis=1, keepdims=True)
    fresh_w = jnp.where(live, jnp.exp(fresh - fresh_top), 0.0)
    fresh_total = jnp.sum(fresh_w, axis=1, keepdims=True)
    fresh_sum = by_head(dot(fresh_w.astype(BF16), vf[...].astype(BF16)))
    emit(qf, q_out)
    emit(kf, k_out)
    emit(vf, v_out)

    def wait1(o):
        peer = lax.rem(me + 1 + o, S)
        came(recv1, send1.at[peer], s1.at[peer], r1, peer, "seq").wait_recv()

    each(S - 1, wait1)
    tops = recv1[:, :, DH : DH + 1]
    sums = recv1[:, :, DH + DH // 2 : DH + DH // 2 + 1]
    high = jnp.maximum(jnp.max(tops, axis=0), fresh_top)
    shrink = jnp.exp(tops - high[None])
    fresh_shrink = jnp.exp(fresh_top - high)
    whole = jnp.sum(sums * shrink, axis=0) + fresh_total * fresh_shrink
    context = jnp.sum(recv1[:, :, :DH] * shrink, axis=0) + fresh_sum * fresh_shrink
    context = context / whole
    context = context.astype(BF16).astype(F32)
    own_cols = iota((pack, cols), 1) // DH == lax.rem(iota((pack, cols), 0), heads)
    tiled = jnp.where(own_cols, jnp.concatenate([context] * heads, axis=1), 0.0)

    def lift(pieces, columns):
        at = iota((8, columns), 0)
        out = jnp.zeros((8, columns), F32)
        for i, piece in enumerate(pieces):
            out = jnp.where(at == i, piece, out)
        return out

    tiled_row = iota((pack, cols), 0) // heads
    flat = lift(
        [
            jnp.sum(jnp.where(tiled_row == i, tiled, 0.0), axis=0, keepdims=True)
            for i in range(own)
        ],
        cols,
    ).astype(BF16)
    out_copy.wait()
    half = width // HALVES

    def copy2(p, peer):
        return pltpu.make_async_remote_copy(
            send2.at[p], recv2.at[p, mp], s2.at[p, peer], r2.at[p, mp],
            device_id={"mp": peer}, device_id_type=MESH,
        )

    others = sorted(range(1, M), key=lambda o: abs(o - M // 2))
    for p in range(HALVES):
        send2[p] = dot(flat, wout[:, p * half : (p + 1) * half])[:own]
        for o in others:
            copy2(p, lax.rem(mp + o, M)).start()
        recv2[p, mp] = send2[p]
    pick = (
        (iota((8, rows), 1) == me * own + iota((8, rows), 0)) & (iota((8, rows), 0) < own)
    ).astype(F32).astype(BF16)
    mine_x = dot(pick, x.astype(BF16))

    def landed2(p, peer):
        return pltpu.make_async_remote_copy(
            send2.at[p], recv2.at[p, peer], s2.at[p, peer], r2.at[p, peer],
            device_id={"mp": peer}, device_id_type=MESH,
        )

    lifted = []
    for p in range(HALVES):
        for o in others:
            landed2(p, lax.rem(mp + o, M)).wait_recv()
        attn = recv2[p, 0]
        for j in range(1, M):
            attn = attn + recv2[p, j]
        lifted.append(lift([attn[i : i + 1] for i in range(own)], half))
    middle = mine_x + jnp.concatenate(lifted, axis=1)
    normed_mid = layer_norm(middle).astype(BF16)
    for j in range(M):
        mids[j] = middle[:own, j * cols : (j + 1) * cols]
    gate_copy.wait()
    gate = dot(normed_mid, wgu[0])
    up_copy.wait()
    up = dot(normed_mid, wgu[1])
    active = (gate / (1.0 + jnp.exp(-gate)) * up).astype(BF16)
    down_copy.wait()

    def copy3(seq, j):
        return pltpu.make_async_remote_copy(
            send3.at[j], recv3.at[me, mp], s3.at[seq, j], r3.at[me, mp],
            device_id={"seq": seq, "mp": j}, device_id_type=MESH,
        )

    def came3(seq, j):
        return pltpu.make_async_remote_copy(
            send3.at[j], recv3.at[seq, j], s3.at[seq, j], r3.at[seq, j],
            device_id={"seq": seq, "mp": j}, device_id_type=MESH,
        )

    def down_block(j):
        return dot(active, wdown[:, pl.ds(pl.multiple_of(j * cols, cols), cols)])[:own]

    def all_blocks(act):
        for o in others:
            j = lax.rem(mp + o, M)
            each(S, lambda i: act(lax.rem(me + S // 2 + i, S), j))
        each(S - 1, lambda i: act(lax.rem(me + 1 + i, S), mp))

    for o in others:
        j = lax.rem(mp + o, M)
        send3[j] = down_block(j)
        each(S, lambda i: copy3(lax.rem(me + S // 2 + i, S), j).start())
    send3[mp] = down_block(mp) + mids[mp]
    each(S - 1, lambda i: copy3(lax.rem(me + 1 + i, S), mp).start())
    recv3[me, mp] = send3[mp]
    all_blocks(lambda seq, j: came3(seq, j).wait_recv())
    for i in range(S):
        hidden = recv3[i, 0]
        for j in range(1, M):
            hidden = hidden + recv3[i, j]
        hf[i * own : (i + 1) * own, :] = hidden
    emit(hf, h_out)

    each(S - 1, lambda o: copy1(lax.rem(me + 1 + o, S)).wait_send())
    for p in range(HALVES):
        for o in others:
            copy2(p, lax.rem(mp + o, M)).wait_send()
    all_blocks(lambda seq, j: copy3(seq, j).wait_send())


def deliver(*refs):
    sems = refs[-1]
    count = len(refs) // 2
    copies = [
        pltpu.make_async_copy(refs[i], refs[count + i], sems.at[i]) for i in range(count)
    ]
    for copy in copies:
        copy.start()
    for copy in copies:
        copy.wait()


def per_device(S, M, inputs, w_qkv, w_out, w_gate_up, w_down, cache_keys, cache_values, lengths):
    batch, steps, width = inputs.shape
    rows = batch * steps
    cols = w_qkv.shape[2]
    heads = cols // DH
    own = rows // S
    pack = own * heads
    anywhere = pl.BlockSpec(memory_space=pl.ANY)
    vmem = pl.BlockSpec(memory_space=pltpu.VMEM)
    shape = (batch, steps, cols)
    small = pltpu.VMEM((rows, cols), F32)
    dma = pltpu.SemaphoreType.DMA
    results = pl.pallas_call(
        functools.partial(kernel, S, M),
        out_shape=[pltpu.VMEM(shape, BF16)] * 4,
        in_specs=[anywhere] * 8,
        out_specs=[vmem] * 4,
        scratch_shapes=[
            pltpu.SMEM(lengths.shape, jnp.int32),
            pltpu.VMEM(inputs.shape, BF16),
            small,
            small,
            small,
            small,
            pltpu.VMEM((S, pack, cols), F32),
            pltpu.VMEM(w_qkv.shape, BF16),
            pltpu.VMEM(w_out.shape, BF16),
            pltpu.VMEM(w_gate_up.shape, BF16),
            pltpu.VMEM(w_down.shape, BF16),
            pltpu.VMEM(cache_keys.shape, BF16),
            pltpu.VMEM(cache_values.shape, BF16),
            pltpu.VMEM((rows, width), F32),
            pltpu.VMEM((S, pack, 2 * DH), F32),
            pltpu.VMEM((S, pack, 2 * DH), F32),
            pltpu.VMEM((HALVES, own, width // HALVES), F32),
            pltpu.VMEM((HALVES, M, own, width // HALVES), F32),
            pltpu.VMEM((M, own, cols), F32),
            pltpu.VMEM((S, M, own, cols), F32),
            pltpu.VMEM((M, own, cols), F32),
            dma((2,)),
            dma((3, QKV_CUTS)),
            dma((4,)),
            dma((2,)),
            dma((S,)),
            dma((S,)),
            dma((HALVES, M)),
            dma((HALVES, M)),
            dma((S, M)),
            dma((S, M)),
        ],
        compiler_params=pltpu.CompilerParams(
            collective_id=0, has_side_effects=True, vmem_limit_bytes=60 * 1024 * 1024
        ),
        name="layer",
    )(lengths, inputs, w_qkv, w_out, w_gate_up, w_down, cache_keys, cache_values)
    queries, keys, values, hidden = (
        pltpu.with_memory_space_constraint(a, pltpu.VMEM) for a in results
    )
    return tuple(
        pl.pallas_call(
            deliver,
            out_shape=[jax.ShapeDtypeStruct(shape, BF16)] * 4,
            in_specs=[vmem] * 4,
            out_specs=[anywhere] * 4,
            scratch_shapes=[dma((4,))],
            name="deliver",
        )(hidden, queries, keys, values)
    )


def solution(mesh):
    cut = P(None, None, "mp")
    cache = P(None, "seq", "mp")
    return jax.shard_map(
        functools.partial(per_device, mesh.shape["seq"], mesh.shape["mp"]),
        mesh=mesh,
        in_specs=(P(), cut, P("mp", None), cut, P("mp", None), cache, cache, P()),
        out_specs=(cut,) * 4,
        check_vma=False,
    )
```

```python
import functools
import math

import jax
import jax.numpy as jnp
from jax import lax
from jax.experimental import pallas as pl
from jax.experimental.pallas import tpu as pltpu
from jax.sharding import PartitionSpec as P

DH = 128
NEG = -1e30
EPS = 1e-05
BASE = 10000.0
MESH = pl.DeviceIdType.MESH
F32 = jnp.float32
BF16 = jnp.bfloat16
QKV_CUTS = 4
HALVES = 2


def each(count, body):
    if count <= 8:
        for i in range(count):
            body(i)
    else:
        lax.fori_loop(0, count, lambda i, c: (body(i), c)[1], 0)


def iota(shape, axis):
    return lax.broadcasted_iota(jnp.int32, shape, axis)


def layer_norm(values):
    average = jnp.mean(values, axis=-1, keepdims=True)
    centred = values - average
    variance = jnp.mean(centred * centred, axis=-1, keepdims=True)
    return centred * lax.rsqrt(variance + EPS)


def split3(value):
    high = value.astype(BF16).astype(F32)
    middle = (value - high).astype(BF16).astype(F32)
    return [high, middle, value - high - middle]


def dot(a, b):
    return jnp.dot(a, b, preferred_element_type=F32)


def kernel(
    S, M,
    len_hbm, x_hbm, wqkv_hbm, wout_hbm, wgu_hbm, wdown_hbm, ck_hbm, cv_hbm,
    q_out, k_out, v_out, h_out,
    len_ref, x_in, qf, kf, vf, hf, wides, wqkv, wout, wgu, wdown, ck, cv,
    xf, send1, recv1, send2, recv2, send3, recv3, mids,
    xsem, qsem, wsem, csem, s1, r1, s2, r2, s3, r3,
):
    batch, steps, width = x_in.shape
    rows = batch * steps
    block = ck.shape[1]
    cols = wqkv.shape[2]
    heads = cols // DH
    own = rows // S
    pack = own * heads
    me = lax.axis_index("seq")
    mp = lax.axis_index("mp")

    x_copy = pltpu.make_async_copy(x_hbm, x_in, xsem.at[0])
    len_copy = pltpu.make_async_copy(len_hbm, len_ref, xsem.at[1])
    x_copy.start()
    len_copy.start()
    cut = width // QKV_CUTS
    q_copies = [
        [
            pltpu.make_async_copy(
                wqkv_hbm.at[j, pl.ds(c * cut, cut)], wqkv.at[j, pl.ds(c * cut, cut)], qsem.at[j, c]
            )
            for c in range(QKV_CUTS)
        ]
        for j in range(3)
    ]
    for c in range(QKV_CUTS):
        q_copies[0][c].start()
    ck_copy = pltpu.make_async_copy(ck_hbm, ck, csem.at[0])
    cv_copy = pltpu.make_async_copy(cv_hbm, cv, csem.at[1])
    ck_copy.start()
    cv_copy.start()
    out_copy = pltpu.make_async_copy(wout_hbm, wout, wsem.at[0])
    gate_copy = pltpu.make_async_copy(wgu_hbm.at[0], wgu.at[0], wsem.at[1])
    up_copy = pltpu.make_async_copy(wgu_hbm.at[1], wgu.at[1], wsem.at[2])
    down_copy = pltpu.make_async_copy(wdown_hbm, wdown, wsem.at[3])

    barrier = pltpu.get_barrier_semaphore()

    def greet(o):
        at = lax.rem(me * M + mp + 1 + o, S * M)
        pl.semaphore_signal(
            barrier, inc=1, device_id={"seq": at // M, "mp": lax.rem(at, M)}, device_id_type=MESH
        )

    if S * M <= 32:
        for o in range(S * M - 1):
            greet(o)
    else:
        each(S * M - 1, greet)

    x_copy.wait()
    for r in range(batch):
        xf[r * steps : (r + 1) * steps, :] = x_in[r].astype(F32)
    x = xf[...]
    normed = layer_norm(x).astype(BF16)

    def project(j):
        total = None
        for c in range(QKV_CUTS):
            q_copies[j][c].wait()
            if j == 0:
                q_copies[1][c].start()
                q_copies[2][c].start()
            term = dot(normed[:, c * cut : (c + 1) * cut], wqkv[j, c * cut : (c + 1) * cut, :])
            total = term if total is None else total + term
        return total

    len_copy.wait()
    token = iota((rows, DH), 0)
    position = lax.rem(token, steps)
    for r in range(batch):
        position = position + jnp.where(token // steps == r, len_ref[r], 0)
    lane = iota((rows, DH), 1)
    fold = lax.rem(lane, DH // 2).astype(F32)
    angle = position.astype(F32) * jnp.exp(fold * (-2.0 * math.log(BASE) / DH))
    cos = jnp.cos(angle)
    sin = jnp.sin(angle)
    sin = jnp.where(lane < DH // 2, -sin, sin)

    def rope(values, ref):
        for h in range(heads):
            v = values[:, h * DH : (h + 1) * DH]
            turned = pltpu.roll(v, DH // 2, 1)
            ref[:, h * DH : (h + 1) * DH] = (v * cos + turned * sin).astype(BF16).astype(F32)

    def emit(ref, out):
        for r in range(batch):
            out[r] = ref[r * steps : (r + 1) * steps, :].astype(BF16)

    rope(project(0), qf)

    full = rows * heads
    spread = (iota((full, rows), 0) // heads == iota((full, rows), 1)).astype(F32).astype(BF16)
    wide = dot(spread, qf[...].astype(BF16))
    own_cols = iota((full, cols), 1) // DH == lax.rem(iota((full, cols), 0), heads)
    wide = jnp.where(own_cols, wide, 0.0)
    wides[...] = wide.reshape(S, pack, cols)
    wide = wide.astype(BF16)

    nt = (((1,), (1,)), ((), ()))
    scale = DH ** -0.5
    group = steps * heads
    ck_copy.wait()
    out_copy.start()
    parts = []
    for r in range(batch):
        raw = lax.dot_general(
            wide[r * group : (r + 1) * group], ck[r], nt, preferred_element_type=F32
        )
        place = iota((group, block), 1) + me * block
        parts.append(jnp.where(place < len_ref[r], raw * scale, NEG))
    scores = jnp.concatenate(parts, axis=0)
    top = jnp.max(scores, axis=1, keepdims=True)
    weights = jnp.where(scores > 0.5 * NEG, jnp.exp(scores - top), 0.0)
    total = jnp.sum(weights, axis=1, keepdims=True)
    cv_copy.wait()
    gate_copy.start()
    weights = weights.astype(BF16)
    summed = jnp.concatenate(
        [dot(weights[r * group : (r + 1) * group], cv[r]) for r in range(batch)], axis=0
    )

    def by_head(wide_rows):
        head_of = lax.rem(iota((wide_rows.shape[0], DH), 0), heads)
        out = jnp.zeros((wide_rows.shape[0], DH), F32)
        for h in range(heads):
            out = out + jnp.where(head_of == h, wide_rows[:, h * DH : (h + 1) * DH], 0.0)
        return out

    spot = iota((full, DH), 1)
    stats = jnp.zeros((full, DH), F32)
    for i, piece in enumerate(split3(top) + split3(total)):
        stats = jnp.where(spot == i, piece, stats)
    send1[:, :, :DH] = by_head(summed).reshape(S, pack, DH).astype(BF16)
    send1[:, :, DH:] = stats.reshape(S, pack, DH).astype(BF16)

    pl.semaphore_wait(barrier, S * M - 1)

    def copy1(peer):
        return pltpu.make_async_remote_copy(
            send1.at[peer], recv1.at[me], s1.at[peer], r1.at[me],
            device_id={"seq": peer}, device_id_type=MESH,
        )

    def came(buf, src, send_sem, recv_sem, slot, axis):
        return pltpu.make_async_remote_copy(
            src, buf.at[slot], send_sem, recv_sem.at[slot],
            device_id={axis: slot}, device_id_type=MESH,
        )

    each(S - 1, lambda o: copy1(lax.rem(me + 1 + o, S)).start())
    recv1[me] = send1[me]

    up_copy.start()
    keys = project(1)
    down_copy.start()
    rope(keys, kf)
    values = project(2)
    vf[...] = values.astype(BF16).astype(F32)
    fresh = (
        lax.dot_general(
            wides[me].astype(BF16), kf[...].astype(BF16), nt, preferred_element_type=F32
        )
        * scale
    )
    row = me * pack + iota((pack, rows), 0)
    col = iota((pack, rows), 1)
    live = (row // group == col // steps) & (lax.rem(col, steps) <= lax.rem(row // heads, steps))
    fresh = jnp.where(live, fresh, NEG)
    fresh_top = jnp.max(fresh, axis=1, keepdims=True)
    fresh_w = jnp.where(live, jnp.exp(fresh - fresh_top), 0.0)
    fresh_total = jnp.sum(fresh_w, axis=1, keepdims=True)
    fresh_sum = by_head(dot(fresh_w.astype(BF16), vf[...].astype(BF16)))
    emit(qf, q_out)
    emit(kf, k_out)
    emit(vf, v_out)

    def wait1(o):
        peer = lax.rem(me + 1 + o, S)
        came(recv1, send1.at[peer], s1.at[peer], r1, peer, "seq").wait_recv()

    each(S - 1, wait1)
    stats = recv1[:, :, DH:].astype(F32)
    tops = stats[:, :, 0:1] + stats[:, :, 1:2] + stats[:, :, 2:3]
    sums = stats[:, :, 3:4] + stats[:, :, 4:5] + stats[:, :, 5:6]
    high = jnp.maximum(jnp.max(tops, axis=0), fresh_top)
    shrink = jnp.exp(tops - high[None])
    fresh_shrink = jnp.exp(fresh_top - high)
    whole = jnp.sum(sums * shrink, axis=0) + fresh_total * fresh_shrink
    context = jnp.sum(recv1[:, :, :DH].astype(F32) * shrink, axis=0) + fresh_sum * fresh_shrink
    context = context / whole
    context = context.astype(BF16).astype(F32)
    own_cols = iota((pack, cols), 1) // DH == lax.rem(iota((pack, cols), 0), heads)
    tiled = jnp.where(own_cols, jnp.concatenate([context] * heads, axis=1), 0.0)

    def lift(pieces, columns):
        at = iota((8, columns), 0)
        out = jnp.zeros((8, columns), F32)
        for i, piece in enumerate(pieces):
            out = jnp.where(at == i, piece, out)
        return out

    tiled_row = iota((pack, cols), 0) // heads
    flat = lift(
        [
            jnp.sum(jnp.where(tiled_row == i, tiled, 0.0), axis=0, keepdims=True)
            for i in range(own)
        ],
        cols,
    ).astype(BF16)
    out_copy.wait()
    half = width // HALVES

    def copy2(p, peer):
        return pltpu.make_async_remote_copy(
            send2.at[p], recv2.at[p, mp], s2.at[p, peer], r2.at[p, mp],
            device_id={"mp": peer}, device_id_type=MESH,
        )

    others = sorted(range(1, M), key=lambda o: abs(o - M // 2))
    for p in range(HALVES):
        send2[p] = dot(flat, wout[:, p * half : (p + 1) * half])[:own].astype(BF16)
        for o in others:
            copy2(p, lax.rem(mp + o, M)).start()
        recv2[p, mp] = send2[p]
    pick = (
        (iota((8, rows), 1) == me * own + iota((8, rows), 0)) & (iota((8, rows), 0) < own)
    ).astype(F32).astype(BF16)
    mine_x = dot(pick, x.astype(BF16))

    def landed2(p, peer):
        return pltpu.make_async_remote_copy(
            send2.at[p], recv2.at[p, peer], s2.at[p, peer], r2.at[p, peer],
            device_id={"mp": peer}, device_id_type=MESH,
        )

    lifted = []
    for p in range(HALVES):
        for o in others:
            landed2(p, lax.rem(mp + o, M)).wait_recv()
        attn = recv2[p, 0].astype(F32)
        for j in range(1, M):
            attn = attn + recv2[p, j].astype(F32)
        lifted.append(lift([attn[i : i + 1] for i in range(own)], half))
    middle = mine_x + jnp.concatenate(lifted, axis=1)
    normed_mid = layer_norm(middle).astype(BF16)
    for j in range(M):
        mids[j] = middle[:own, j * cols : (j + 1) * cols]
    gate_copy.wait()
    gate = dot(normed_mid, wgu[0])
    up_copy.wait()
    up = dot(normed_mid, wgu[1])
    active = (gate / (1.0 + jnp.exp(-gate)) * up).astype(BF16)
    down_copy.wait()

    def copy3(seq, j):
        return pltpu.make_async_remote_copy(
            send3.at[j], recv3.at[me, mp], s3.at[seq, j], r3.at[me, mp],
            device_id={"seq": seq, "mp": j}, device_id_type=MESH,
        )

    def came3(seq, j):
        return pltpu.make_async_remote_copy(
            send3.at[j], recv3.at[seq, j], s3.at[seq, j], r3.at[seq, j],
            device_id={"seq": seq, "mp": j}, device_id_type=MESH,
        )

    def down_block(j):
        return dot(active, wdown[:, pl.ds(pl.multiple_of(j * cols, cols), cols)])[:own]

    def all_blocks(act):
        for o in others:
            j = lax.rem(mp + o, M)
            each(S, lambda i: act(lax.rem(me + S // 2 + i, S), j))
        each(S - 1, lambda i: act(lax.rem(me + 1 + i, S), mp))

    for o in others:
        j = lax.rem(mp + o, M)
        send3[j] = down_block(j).astype(BF16)
        each(S, lambda i: copy3(lax.rem(me + S // 2 + i, S), j).start())
    send3[mp] = (down_block(mp) + mids[mp]).astype(BF16)
    each(S - 1, lambda i: copy3(lax.rem(me + 1 + i, S), mp).start())
    recv3[me, mp] = send3[mp]
    all_blocks(lambda seq, j: came3(seq, j).wait_recv())
    for i in range(S):
        hidden = recv3[i, 0].astype(F32)
        for j in range(1, M):
            hidden = hidden + recv3[i, j].astype(F32)
        hf[i * own : (i + 1) * own, :] = hidden
    emit(hf, h_out)

    each(S - 1, lambda o: copy1(lax.rem(me + 1 + o, S)).wait_send())
    for p in range(HALVES):
        for o in others:
            copy2(p, lax.rem(mp + o, M)).wait_send()
    all_blocks(lambda seq, j: copy3(seq, j).wait_send())


def deliver(*refs):
    sems = refs[-1]
    count = len(refs) // 2
    copies = [
        pltpu.make_async_copy(refs[i], refs[count + i], sems.at[i]) for i in range(count)
    ]
    for copy in copies:
        copy.start()
    for copy in copies:
        copy.wait()


def per_device(S, M, inputs, w_qkv, w_out, w_gate_up, w_down, cache_keys, cache_values, lengths):
    batch, steps, width = inputs.shape
    rows = batch * steps
    cols = w_qkv.shape[2]
    heads = cols // DH
    own = rows // S
    pack = own * heads
    anywhere = pl.BlockSpec(memory_space=pl.ANY)
    vmem = pl.BlockSpec(memory_space=pltpu.VMEM)
    shape = (batch, steps, cols)
    small = pltpu.VMEM((rows, cols), F32)
    dma = pltpu.SemaphoreType.DMA
    results = pl.pallas_call(
        functools.partial(kernel, S, M),
        out_shape=[pltpu.VMEM(shape, BF16)] * 4,
        in_specs=[anywhere] * 8,
        out_specs=[vmem] * 4,
        scratch_shapes=[
            pltpu.SMEM(lengths.shape, jnp.int32),
            pltpu.VMEM(inputs.shape, BF16),
            small,
            small,
            small,
            small,
            pltpu.VMEM((S, pack, cols), F32),
            pltpu.VMEM(w_qkv.shape, BF16),
            pltpu.VMEM(w_out.shape, BF16),
            pltpu.VMEM(w_gate_up.shape, BF16),
            pltpu.VMEM(w_down.shape, BF16),
            pltpu.VMEM(cache_keys.shape, BF16),
            pltpu.VMEM(cache_values.shape, BF16),
            pltpu.VMEM((rows, width), F32),
            pltpu.VMEM((S, pack, 2 * DH), BF16),
            pltpu.VMEM((S, pack, 2 * DH), BF16),
            pltpu.VMEM((HALVES, own, width // HALVES), BF16),
            pltpu.VMEM((HALVES, M, own, width // HALVES), BF16),
            pltpu.VMEM((M, own, cols), BF16),
            pltpu.VMEM((S, M, own, cols), BF16),
            pltpu.VMEM((M, own, cols), F32),
            dma((2,)),
            dma((3, QKV_CUTS)),
            dma((4,)),
            dma((2,)),
            dma((S,)),
            dma((S,)),
            dma((HALVES, M)),
            dma((HALVES, M)),
            dma((S, M)),
            dma((S, M)),
        ],
        compiler_params=pltpu.CompilerParams(
            collective_id=0, has_side_effects=True, vmem_limit_bytes=60 * 1024 * 1024
        ),
        name="layer",
    )(lengths, inputs, w_qkv, w_out, w_gate_up, w_down, cache_keys, cache_values)
    queries, keys, values, hidden = (
        pltpu.with_memory_space_constraint(a, pltpu.VMEM) for a in results
    )
    return tuple(
        pl.pallas_call(
            deliver,
            out_shape=[jax.ShapeDtypeStruct(shape, BF16)] * 4,
            in_specs=[vmem] * 4,
            out_specs=[anywhere] * 4,
            scratch_shapes=[dma((4,))],
            name="deliver",
        )(hidden, queries, keys, values)
    )


def solution(mesh):
    cut = P(None, None, "mp")
    cache = P(None, "seq", "mp")
    return jax.shard_map(
        functools.partial(per_device, mesh.shape["seq"], mesh.shape["mp"]),
        mesh=mesh,
        in_specs=(P(), cut, P("mp", None), cut, P("mp", None), cache, cache, P()),
        out_specs=(cut,) * 4,
        check_vma=False,
    )
```

```python
import functools
import math

import jax
import jax.numpy as jnp
from jax import lax
from jax.experimental import pallas as pl
from jax.experimental.pallas import tpu as pltpu
from jax.sharding import PartitionSpec as P

DH = 128
NEG = -1e30
EPS = 1e-05
BASE = 10000.0
MESH = pl.DeviceIdType.MESH
F32 = jnp.float32
BF16 = jnp.bfloat16
QKV_CUTS = 4
HALVES = 2
PAIR = 2


def each(count, body):
    if count <= 8:
        for i in range(count):
            body(i)
    else:
        lax.fori_loop(0, count, lambda i, c: (body(i), c)[1], 0)


def iota(shape, axis):
    return lax.broadcasted_iota(jnp.int32, shape, axis)


def layer_norm(values):
    average = jnp.mean(values, axis=-1, keepdims=True)
    centred = values - average
    variance = jnp.mean(centred * centred, axis=-1, keepdims=True)
    return centred * lax.rsqrt(variance + EPS)


def split3(value):
    high = value.astype(BF16).astype(F32)
    middle = (value - high).astype(BF16).astype(F32)
    return [high, middle, value - high - middle]


def dot(a, b):
    return jnp.dot(a, b, preferred_element_type=F32)


def kernel(
    S, M,
    len_hbm, x_hbm, wqkv_hbm, wout_hbm, wgu_hbm, wdown_hbm, ck_hbm, cv_hbm,
    q_out, k_out, v_out, h_out,
    len_ref, x_in, qf, kf, vf, hf, wides, wqkv, wout, wgu, wdown, ck, cv,
    xf, send1, recv1, send2, recv2, send3, recv3, mids,
    xsem, qsem, wsem, csem, s1, r1, s2, r2, s3, r3,
):
    batch, steps, width = x_in.shape
    rows = batch * steps
    block = ck.shape[1]
    cols = wqkv.shape[2]
    heads = cols // DH
    own = rows // S
    pack = own * heads
    team = own * PAIR
    few = heads // PAIR
    hidden_units = wdown.shape[0]
    me = lax.axis_index("seq")
    mp = lax.axis_index("mp")
    unit = lax.rem(me, PAIR)
    first = me - unit

    x_copy = pltpu.make_async_copy(x_hbm, x_in, xsem.at[0])
    len_copy = pltpu.make_async_copy(len_hbm, len_ref, xsem.at[1])
    x_copy.start()
    len_copy.start()
    cut = width // QKV_CUTS
    q_copies = [
        [
            pltpu.make_async_copy(
                wqkv_hbm.at[j, pl.ds(c * cut, cut)], wqkv.at[j, pl.ds(c * cut, cut)], qsem.at[j, c]
            )
            for c in range(QKV_CUTS)
        ]
        for j in range(3)
    ]
    for c in range(QKV_CUTS):
        q_copies[0][c].start()
    ck_copy = pltpu.make_async_copy(ck_hbm, ck, csem.at[0])
    cv_copy = pltpu.make_async_copy(cv_hbm, cv, csem.at[1])
    ck_copy.start()
    cv_copy.start()
    unit_cols = pl.ds(pl.multiple_of(unit * hidden_units, hidden_units), hidden_units)
    out_copy = pltpu.make_async_copy(
        wout_hbm.at[pl.ds(unit * few * DH, few * DH)], wout, wsem.at[0])
    gate_copy = pltpu.make_async_copy(
        wgu_hbm.at[0, :, unit_cols], wgu.at[0], wsem.at[1])
    up_copy = pltpu.make_async_copy(
        wgu_hbm.at[1, :, unit_cols], wgu.at[1], wsem.at[2])
    down_copy = pltpu.make_async_copy(
        wdown_hbm.at[pl.ds(unit * hidden_units, hidden_units)], wdown, wsem.at[3])

    barrier = pltpu.get_barrier_semaphore()

    def greet(o):
        at = lax.rem(me * M + mp + 1 + o, S * M)
        pl.semaphore_signal(
            barrier, inc=1, device_id={"seq": at // M, "mp": lax.rem(at, M)}, device_id_type=MESH
        )

    if S * M <= 32:
        for o in range(S * M - 1):
            greet(o)
    else:
        each(S * M - 1, greet)

    x_copy.wait()
    for r in range(batch):
        xf[r * steps : (r + 1) * steps, :] = x_in[r].astype(F32)
    x = xf[...]
    normed = layer_norm(x).astype(BF16)

    def project(j):
        total = None
        for c in range(QKV_CUTS):
            q_copies[j][c].wait()
            if j == 0:
                q_copies[1][c].start()
                q_copies[2][c].start()
            term = dot(normed[:, c * cut : (c + 1) * cut], wqkv[j, c * cut : (c + 1) * cut, :])
            total = term if total is None else total + term
        return total

    len_copy.wait()
    token = iota((rows, DH), 0)
    position = lax.rem(token, steps)
    for r in range(batch):
        position = position + jnp.where(token // steps == r, len_ref[r], 0)
    lane = iota((rows, DH), 1)
    fold = lax.rem(lane, DH // 2).astype(F32)
    angle = position.astype(F32) * jnp.exp(fold * (-2.0 * math.log(BASE) / DH))
    cos = jnp.cos(angle)
    sin = jnp.sin(angle)
    sin = jnp.where(lane < DH // 2, -sin, sin)

    def rope(values, ref):
        for h in range(heads):
            v = values[:, h * DH : (h + 1) * DH]
            turned = pltpu.roll(v, DH // 2, 1)
            ref[:, h * DH : (h + 1) * DH] = (v * cos + turned * sin).astype(BF16).astype(F32)

    def emit(ref, out):
        for r in range(batch):
            out[r] = ref[r * steps : (r + 1) * steps, :].astype(BF16)

    rope(project(0), qf)

    full = rows * heads

    def token_of(row):
        return row // (PAIR * pack) * team + lax.rem(row, pack) // few

    def head_of(row):
        return lax.rem(row // pack, PAIR) * few + lax.rem(row, few)

    spread = (token_of(iota((full, rows), 0)) == iota((full, rows), 1)).astype(F32).astype(BF16)
    wide = dot(spread, qf[...].astype(BF16))
    own_cols = iota((full, cols), 1) // DH == head_of(iota((full, cols), 0))
    wide = jnp.where(own_cols, wide, 0.0)
    wides[...] = wide.reshape(S, pack, cols)
    wide = wide.astype(BF16)

    nt = (((1,), (1,)), ((), ()))
    scale = DH ** -0.5
    group = steps * heads
    ck_copy.wait()
    out_copy.start()
    parts = []
    for r in range(batch):
        raw = lax.dot_general(
            wide[r * group : (r + 1) * group], ck[r], nt, preferred_element_type=F32
        )
        place = iota((group, block), 1) + me * block
        parts.append(jnp.where(place < len_ref[r], raw * scale, NEG))
    scores = jnp.concatenate(parts, axis=0)
    top = jnp.max(scores, axis=1, keepdims=True)
    weights = jnp.where(scores > 0.5 * NEG, jnp.exp(scores - top), 0.0)
    total = jnp.sum(weights, axis=1, keepdims=True)
    cv_copy.wait()
    gate_copy.start()
    weights = weights.astype(BF16)
    summed = jnp.concatenate(
        [dot(weights[r * group : (r + 1) * group], cv[r]) for r in range(batch)], axis=0
    )

    def by_head(wide_rows, start):
        head = head_of(start + iota((wide_rows.shape[0], DH), 0))
        out = jnp.zeros((wide_rows.shape[0], DH), F32)
        for h in range(heads):
            out = out + jnp.where(head == h, wide_rows[:, h * DH : (h + 1) * DH], 0.0)
        return out

    spot = iota((full, DH), 1)
    stats = jnp.zeros((full, DH), F32)
    for i, piece in enumerate(split3(top) + split3(total)):
        stats = jnp.where(spot == i, piece, stats)
    send1[:, :, :DH] = by_head(summed, 0).reshape(S, pack, DH).astype(BF16)
    send1[:, :, DH:] = stats.reshape(S, pack, DH).astype(BF16)

    pl.semaphore_wait(barrier, S * M - 1)

    def copy1(peer):
        return pltpu.make_async_remote_copy(
            send1.at[peer], recv1.at[me], s1.at[peer], r1.at[me],
            device_id={"seq": peer}, device_id_type=MESH,
        )

    def came(buf, src, send_sem, recv_sem, slot, axis):
        return pltpu.make_async_remote_copy(
            src, buf.at[slot], send_sem, recv_sem.at[slot],
            device_id={axis: slot}, device_id_type=MESH,
        )

    each(S - 1, lambda o: copy1(lax.rem(me + 1 + o, S)).start())
    recv1[me] = send1[me]

    up_copy.start()
    keys = project(1)
    down_copy.start()
    rope(keys, kf)
    values = project(2)
    vf[...] = values.astype(BF16).astype(F32)
    fresh = (
        lax.dot_general(
            wides[me].astype(BF16), kf[...].astype(BF16), nt, preferred_element_type=F32
        )
        * scale
    )
    row = token_of(me * pack + iota((pack, rows), 0))
    col = iota((pack, rows), 1)
    live = (row // steps == col // steps) & (col <= row)
    fresh = jnp.where(live, fresh, NEG)
    fresh_top = jnp.max(fresh, axis=1, keepdims=True)
    fresh_w = jnp.where(live, jnp.exp(fresh - fresh_top), 0.0)
    fresh_total = jnp.sum(fresh_w, axis=1, keepdims=True)
    fresh_sum = by_head(dot(fresh_w.astype(BF16), vf[...].astype(BF16)), me * pack)
    emit(qf, q_out)
    emit(kf, k_out)
    emit(vf, v_out)

    def wait1(o):
        peer = lax.rem(me + 1 + o, S)
        came(recv1, send1.at[peer], s1.at[peer], r1, peer, "seq").wait_recv()

    each(S - 1, wait1)
    stats = recv1[:, :, DH:].astype(F32)
    tops = stats[:, :, 0:1] + stats[:, :, 1:2] + stats[:, :, 2:3]
    sums = stats[:, :, 3:4] + stats[:, :, 4:5] + stats[:, :, 5:6]
    high = jnp.maximum(jnp.max(tops, axis=0), fresh_top)
    shrink = jnp.exp(tops - high[None])
    fresh_shrink = jnp.exp(fresh_top - high)
    whole = jnp.sum(sums * shrink, axis=0) + fresh_total * fresh_shrink
    context = jnp.sum(recv1[:, :, :DH].astype(F32) * shrink, axis=0) + fresh_sum * fresh_shrink
    context = context / whole
    context = context.astype(BF16).astype(F32)
    part_cols = few * DH
    own_cols = iota((pack, part_cols), 1) // DH == lax.rem(iota((pack, part_cols), 0), few)
    tiled = jnp.where(own_cols, jnp.concatenate([context] * few, axis=1), 0.0)

    def lift(pieces, columns):
        at = iota((8, columns), 0)
        out = jnp.zeros((8, columns), F32)
        for i, piece in enumerate(pieces):
            out = jnp.where(at == i, piece, out)
        return out

    tiled_row = iota((pack, part_cols), 0) // few
    flat = lift(
        [
            jnp.sum(jnp.where(tiled_row == i, tiled, 0.0), axis=0, keepdims=True)
            for i in range(team)
        ],
        part_cols,
    ).astype(BF16)
    out_copy.wait()
    half = width // HALVES

    def copy2(p, u, j):
        return pltpu.make_async_remote_copy(
            send2.at[p], recv2.at[p, unit, mp], s2.at[p, u, j], r2.at[p, unit, mp],
            device_id={"seq": first + u, "mp": j}, device_id_type=MESH,
        )

    others = sorted(range(1, M), key=lambda o: abs(o - M // 2))
    near = [(v, o) for v in range(PAIR - 1, -1, -1) for o in others] + [(v, 0) for v in range(1, PAIR)]
    near = [(lax.rem(unit + v, PAIR), lax.rem(mp + o, M)) for v, o in near]
    for p in range(HALVES):
        send2[p] = dot(flat, wout[:, p * half : (p + 1) * half])[:team].astype(BF16)
        for u, j in near:
            copy2(p, u, j).start()
        recv2[p, unit, mp] = send2[p]
    pick = (
        (iota((8, rows), 1) == first * own + iota((8, rows), 0))
        & (iota((8, rows), 0) < team)
    ).astype(F32).astype(BF16)
    mine_x = dot(pick, x.astype(BF16))

    def landed2(p, u, j):
        return pltpu.make_async_remote_copy(
            send2.at[p], recv2.at[p, u, j], s2.at[p, u, j], r2.at[p, u, j],
            device_id={"seq": first + u, "mp": j}, device_id_type=MESH,
        )

    lifted = []
    for p in range(HALVES):
        for u, j in near:
            landed2(p, u, j).wait_recv()
        attn = jnp.zeros((team, half), F32)
        for u in range(PAIR):
            for j in range(M):
                attn = attn + recv2[p, u, j].astype(F32)
        lifted.append(lift([attn[i : i + 1] for i in range(team)], half))
    middle = mine_x + jnp.concatenate(lifted, axis=1)
    normed_mid = layer_norm(middle).astype(BF16)
    for j in range(M):
        mids[j] = jnp.where(unit == 0, middle[:team, j * cols : (j + 1) * cols], 0.0)
    gate_copy.wait()
    gate = dot(normed_mid, wgu[0])
    up_copy.wait()
    up = dot(normed_mid, wgu[1])
    active = (gate / (1.0 + jnp.exp(-gate)) * up).astype(BF16)
    down_copy.wait()

    def copy3(seq, j):
        return pltpu.make_async_remote_copy(
            send3.at[j], recv3.at[me, mp], s3.at[seq, j], r3.at[me, mp],
            device_id={"seq": seq, "mp": j}, device_id_type=MESH,
        )

    def came3(seq, j):
        return pltpu.make_async_remote_copy(
            send3.at[j], recv3.at[seq, j], s3.at[seq, j], r3.at[seq, j],
            device_id={"seq": seq, "mp": j}, device_id_type=MESH,
        )

    def down_block(j):
        return dot(active, wdown[:, pl.ds(pl.multiple_of(j * cols, cols), cols)])[:team]

    def all_blocks(act):
        for o in others:
            j = lax.rem(mp + o, M)
            each(S, lambda i: act(lax.rem(me + S // 2 + i, S), j))
        each(S - 1, lambda i: act(lax.rem(me + 1 + i, S), mp))

    for o in others:
        j = lax.rem(mp + o, M)
        send3[j] = down_block(j).astype(BF16)
        each(S, lambda i: copy3(lax.rem(me + S // 2 + i, S), j).start())
    send3[mp] = (down_block(mp) + mids[mp]).astype(BF16)
    each(S - 1, lambda i: copy3(lax.rem(me + 1 + i, S), mp).start())
    recv3[me, mp] = send3[mp]
    all_blocks(lambda seq, j: came3(seq, j).wait_recv())
    for i in range(S // PAIR):
        hidden = jnp.zeros((team, cols), F32)
        for u in range(PAIR):
            for j in range(M):
                hidden = hidden + recv3[i * PAIR + u, j].astype(F32)
        hf[i * team : (i + 1) * team, :] = hidden
    emit(hf, h_out)

    each(S - 1, lambda o: copy1(lax.rem(me + 1 + o, S)).wait_send())
    for p in range(HALVES):
        for u, j in near:
            copy2(p, u, j).wait_send()
    all_blocks(lambda seq, j: copy3(seq, j).wait_send())


def deliver(*refs):
    sems = refs[-1]
    count = len(refs) // 2
    copies = [
        pltpu.make_async_copy(refs[i], refs[count + i], sems.at[i]) for i in range(count)
    ]
    for copy in copies:
        copy.start()
    for copy in copies:
        copy.wait()


def per_device(S, M, inputs, w_qkv, w_out, w_gate_up, w_down, cache_keys, cache_values, lengths):
    batch, steps, width = inputs.shape
    rows = batch * steps
    cols = w_qkv.shape[2]
    heads = cols // DH
    own = rows // S
    pack = own * heads
    team = own * PAIR
    units = w_down.shape[0] // PAIR
    anywhere = pl.BlockSpec(memory_space=pl.ANY)
    vmem = pl.BlockSpec(memory_space=pltpu.VMEM)
    shape = (batch, steps, cols)
    small = pltpu.VMEM((rows, cols), F32)
    dma = pltpu.SemaphoreType.DMA
    results = pl.pallas_call(
        functools.partial(kernel, S, M),
        out_shape=[pltpu.VMEM(shape, BF16)] * 4,
        in_specs=[anywhere] * 8,
        out_specs=[vmem] * 4,
        scratch_shapes=[
            pltpu.SMEM(lengths.shape, jnp.int32),
            pltpu.VMEM(inputs.shape, BF16),
            small,
            small,
            small,
            small,
            pltpu.VMEM((S, pack, cols), F32),
            pltpu.VMEM(w_qkv.shape, BF16),
            pltpu.VMEM((cols // PAIR, width), BF16),
            pltpu.VMEM((2, width, units), BF16),
            pltpu.VMEM((units, width), BF16),
            pltpu.VMEM(cache_keys.shape, BF16),
            pltpu.VMEM(cache_values.shape, BF16),
            pltpu.VMEM((rows, width), F32),
            pltpu.VMEM((S, pack, 2 * DH), BF16),
            pltpu.VMEM((S, pack, 2 * DH), BF16),
            pltpu.VMEM((HALVES, team, width // HALVES), BF16),
            pltpu.VMEM((HALVES, PAIR, M, team, width // HALVES), BF16),
            pltpu.VMEM((M, team, cols), BF16),
            pltpu.VMEM((S, M, team, cols), BF16),
            pltpu.VMEM((M, team, cols), F32),
            dma((2,)),
            dma((3, QKV_CUTS)),
            dma((4,)),
            dma((2,)),
            dma((S,)),
            dma((S,)),
            dma((HALVES, PAIR, M)),
            dma((HALVES, PAIR, M)),
            dma((S, M)),
            dma((S, M)),
        ],
        compiler_params=pltpu.CompilerParams(
            collective_id=0, has_side_effects=True, vmem_limit_bytes=60 * 1024 * 1024
        ),
        name="layer",
    )(lengths, inputs, w_qkv, w_out, w_gate_up, w_down, cache_keys, cache_values)
    queries, keys, values, hidden = (
        pltpu.with_memory_space_constraint(a, pltpu.VMEM) for a in results
    )
    return tuple(
        pl.pallas_call(
            deliver,
            out_shape=[jax.ShapeDtypeStruct(shape, BF16)] * 4,
            in_specs=[vmem] * 4,
            out_specs=[anywhere] * 4,
            scratch_shapes=[dma((4,))],
            name="deliver",
        )(hidden, queries, keys, values)
    )


def solution(mesh):
    cut = P(None, None, "mp")
    cache = P(None, "seq", "mp")
    return jax.shard_map(
        functools.partial(per_device, mesh.shape["seq"], mesh.shape["mp"]),
        mesh=mesh,
        in_specs=(P(), cut, P("mp", None), cut, P("mp", None), cache, cache, P()),
        out_specs=(cut,) * 4,
        check_vma=False,
    )
```

```python
import functools
import math

import jax
import jax.numpy as jnp
from jax import lax
from jax.experimental import pallas as pl
from jax.experimental.pallas import tpu as pltpu
from jax.sharding import PartitionSpec as P

DH = 128
NEG = -1e30
EPS = 1e-05
BASE = 10000.0
MESH = pl.DeviceIdType.MESH
F32 = jnp.float32
BF16 = jnp.bfloat16
QKV_CUTS = 4
HALVES = 1
PAIR = 2


def each(count, body):
    if count <= 8:
        for i in range(count):
            body(i)
    else:
        lax.fori_loop(0, count, lambda i, c: (body(i), c)[1], 0)


def iota(shape, axis):
    return lax.broadcasted_iota(jnp.int32, shape, axis)


def layer_norm(values):
    average = jnp.mean(values, axis=-1, keepdims=True)
    centred = values - average
    variance = jnp.mean(centred * centred, axis=-1, keepdims=True)
    return centred * lax.rsqrt(variance + EPS)


def split3(value):
    high = value.astype(BF16).astype(F32)
    middle = (value - high).astype(BF16).astype(F32)
    return [high, middle, value - high - middle]


def dot(a, b):
    return jnp.dot(a, b, preferred_element_type=F32)


def kernel(
    S, M,
    len_hbm, x_hbm, wqkv_hbm, wout_hbm, wgu_hbm, wdown_hbm, ck_hbm, cv_hbm,
    q_out, k_out, v_out, h_out,
    len_ref, x_in, qf, kf, vf, hf, wides, wqkv, wout, wgu, wdown, ck, cv,
    xf, send1, recv1, send2, recv2, send3, recv3, mids, send4, recv4,
    xsem, qsem, wsem, csem, s1, r1, s2, r2, s3, r3, s4, r4,
):
    batch, steps, width = x_in.shape
    rows = batch * steps
    block = ck.shape[1]
    cols = wqkv.shape[2]
    heads = cols // DH
    own = rows // S
    pack = own * heads
    team = own * PAIR
    few = heads // PAIR
    hidden_units = wdown.shape[0]
    me = lax.axis_index("seq")
    mp = lax.axis_index("mp")
    unit = lax.rem(me, PAIR)
    first = me - unit

    x_copy = pltpu.make_async_copy(x_hbm, x_in, xsem.at[0])
    len_copy = pltpu.make_async_copy(len_hbm, len_ref, xsem.at[1])
    x_copy.start()
    len_copy.start()
    cut = width // QKV_CUTS
    q_copies = [
        [
            pltpu.make_async_copy(
                wqkv_hbm.at[j, pl.ds(c * cut, cut)], wqkv.at[j, pl.ds(c * cut, cut)], qsem.at[j, c]
            )
            for c in range(QKV_CUTS)
        ]
        for j in range(3)
    ]
    for c in range(QKV_CUTS):
        q_copies[0][c].start()
    ck_copy = pltpu.make_async_copy(ck_hbm, ck, csem.at[0])
    cv_copy = pltpu.make_async_copy(cv_hbm, cv, csem.at[1])
    ck_copy.start()
    cv_copy.start()
    unit_cols = pl.ds(pl.multiple_of(unit * hidden_units, hidden_units), hidden_units)
    out_copy = pltpu.make_async_copy(
        wout_hbm.at[pl.ds(unit * few * DH, few * DH)], wout, wsem.at[0])
    gate_copy = pltpu.make_async_copy(
        wgu_hbm.at[0, :, unit_cols], wgu.at[0], wsem.at[1])
    up_copy = pltpu.make_async_copy(
        wgu_hbm.at[1, :, unit_cols], wgu.at[1], wsem.at[2])
    down_copy = pltpu.make_async_copy(
        wdown_hbm.at[pl.ds(unit * hidden_units, hidden_units)], wdown, wsem.at[3])

    barrier = pltpu.get_barrier_semaphore()

    def greet(seq, j):
        pl.semaphore_signal(
            barrier, inc=1, device_id={"seq": seq, "mp": j}, device_id_type=MESH
        )

    each(S - 1, lambda o: greet(lax.rem(me + 1 + o, S), mp))
    for u in range(PAIR):
        for o in range(1, M):
            greet(first + u, lax.rem(mp + o, M))

    x_copy.wait()
    for r in range(batch):
        xf[r * steps : (r + 1) * steps, :] = x_in[r].astype(F32)
    x = xf[...]
    normed = layer_norm(x).astype(BF16)

    def project(j):
        total = None
        for c in range(QKV_CUTS):
            q_copies[j][c].wait()
            if j == 0:
                q_copies[1][c].start()
                q_copies[2][c].start()
            term = dot(normed[:, c * cut : (c + 1) * cut], wqkv[j, c * cut : (c + 1) * cut, :])
            total = term if total is None else total + term
        return total

    len_copy.wait()
    token = iota((rows, DH), 0)
    position = lax.rem(token, steps)
    for r in range(batch):
        position = position + jnp.where(token // steps == r, len_ref[r], 0)
    lane = iota((rows, DH), 1)
    fold = lax.rem(lane, DH // 2).astype(F32)
    angle = position.astype(F32) * jnp.exp(fold * (-2.0 * math.log(BASE) / DH))
    cos = jnp.cos(angle)
    sin = jnp.sin(angle)
    sin = jnp.where(lane < DH // 2, -sin, sin)

    def rope(values, ref):
        for h in range(heads):
            v = values[:, h * DH : (h + 1) * DH]
            turned = pltpu.roll(v, DH // 2, 1)
            ref[:, h * DH : (h + 1) * DH] = (v * cos + turned * sin).astype(BF16).astype(F32)

    def emit(ref, out):
        for r in range(batch):
            out[r] = ref[r * steps : (r + 1) * steps, :].astype(BF16)

    rope(project(0), qf)

    full = rows * heads

    def token_of(row):
        return row // (PAIR * pack) * team + lax.rem(row, pack) // few

    def head_of(row):
        return lax.rem(row // pack, PAIR) * few + lax.rem(row, few)

    spread = (token_of(iota((full, rows), 0)) == iota((full, rows), 1)).astype(F32).astype(BF16)
    wide = dot(spread, qf[...].astype(BF16))
    own_cols = iota((full, cols), 1) // DH == head_of(iota((full, cols), 0))
    wide = jnp.where(own_cols, wide, 0.0)
    wides[...] = wide.reshape(S, pack, cols)
    wide = wide.astype(BF16)

    nt = (((1,), (1,)), ((), ()))
    scale = DH ** -0.5
    group = steps * heads
    ck_copy.wait()
    out_copy.start()
    parts = []
    for r in range(batch):
        raw = lax.dot_general(
            wide[r * group : (r + 1) * group], ck[r], nt, preferred_element_type=F32
        )
        place = iota((group, block), 1) + me * block
        parts.append(jnp.where(place < len_ref[r], raw * scale, NEG))
    scores = jnp.concatenate(parts, axis=0)
    top = jnp.max(scores, axis=1, keepdims=True)
    weights = jnp.where(scores > 0.5 * NEG, jnp.exp(scores - top), 0.0)
    total = jnp.sum(weights, axis=1, keepdims=True)
    cv_copy.wait()
    gate_copy.start()
    weights = weights.astype(BF16)
    summed = jnp.concatenate(
        [dot(weights[r * group : (r + 1) * group], cv[r]) for r in range(batch)], axis=0
    )

    def by_head(wide_rows, start):
        head = head_of(start + iota((wide_rows.shape[0], DH), 0))
        out = jnp.zeros((wide_rows.shape[0], DH), F32)
        for h in range(heads):
            out = out + jnp.where(head == h, wide_rows[:, h * DH : (h + 1) * DH], 0.0)
        return out

    spot = iota((full, DH), 1)
    stats = jnp.zeros((full, DH), F32)
    for i, piece in enumerate(split3(top) + split3(total)):
        stats = jnp.where(spot == i, piece, stats)
    send1[:, :, :DH] = by_head(summed, 0).reshape(S, pack, DH).astype(BF16)
    send1[:, :, DH:] = stats.reshape(S, pack, DH).astype(BF16)

    pl.semaphore_wait(barrier, S - 1 + PAIR * (M - 1))

    def copy1(peer):
        return pltpu.make_async_remote_copy(
            send1.at[peer], recv1.at[me], s1.at[peer], r1.at[me],
            device_id={"seq": peer}, device_id_type=MESH,
        )

    def came(buf, src, send_sem, recv_sem, slot, axis):
        return pltpu.make_async_remote_copy(
            src, buf.at[slot], send_sem, recv_sem.at[slot],
            device_id={axis: slot}, device_id_type=MESH,
        )

    each(S - 1, lambda o: copy1(lax.rem(me + 1 + o, S)).start())
    recv1[me] = send1[me]

    up_copy.start()
    keys = project(1)
    down_copy.start()
    rope(keys, kf)
    values = project(2)
    vf[...] = values.astype(BF16).astype(F32)
    fresh = (
        lax.dot_general(
            wides[me].astype(BF16), kf[...].astype(BF16), nt, preferred_element_type=F32
        )
        * scale
    )
    row = token_of(me * pack + iota((pack, rows), 0))
    col = iota((pack, rows), 1)
    live = (row // steps == col // steps) & (col <= row)
    fresh = jnp.where(live, fresh, NEG)
    fresh_top = jnp.max(fresh, axis=1, keepdims=True)
    fresh_w = jnp.where(live, jnp.exp(fresh - fresh_top), 0.0)
    fresh_total = jnp.sum(fresh_w, axis=1, keepdims=True)
    fresh_sum = by_head(dot(fresh_w.astype(BF16), vf[...].astype(BF16)), me * pack)
    emit(qf, q_out)
    emit(kf, k_out)
    emit(vf, v_out)

    def wait1(o):
        peer = lax.rem(me + 1 + o, S)
        came(recv1, send1.at[peer], s1.at[peer], r1, peer, "seq").wait_recv()

    each(S - 1, wait1)
    stats = recv1[:, :, DH:].astype(F32)
    tops = stats[:, :, 0:1] + stats[:, :, 1:2] + stats[:, :, 2:3]
    sums = stats[:, :, 3:4] + stats[:, :, 4:5] + stats[:, :, 5:6]
    high = jnp.maximum(jnp.max(tops, axis=0), fresh_top)
    shrink = jnp.exp(tops - high[None])
    fresh_shrink = jnp.exp(fresh_top - high)
    whole = jnp.sum(sums * shrink, axis=0) + fresh_total * fresh_shrink
    context = jnp.sum(recv1[:, :, :DH].astype(F32) * shrink, axis=0) + fresh_sum * fresh_shrink
    context = context / whole
    context = context.astype(BF16).astype(F32)
    part_cols = few * DH
    own_cols = iota((pack, part_cols), 1) // DH == lax.rem(iota((pack, part_cols), 0), few)
    tiled = jnp.where(own_cols, jnp.concatenate([context] * few, axis=1), 0.0)

    def lift(pieces, columns):
        at = iota((8, columns), 0)
        out = jnp.zeros((8, columns), F32)
        for i, piece in enumerate(pieces):
            out = jnp.where(at == i, piece, out)
        return out

    tiled_row = iota((pack, part_cols), 0) // few
    flat = lift(
        [
            jnp.sum(jnp.where(tiled_row == i, tiled, 0.0), axis=0, keepdims=True)
            for i in range(team)
        ],
        part_cols,
    ).astype(BF16)
    out_copy.wait()
    half = width // HALVES

    def copy2(p, u, j):
        return pltpu.make_async_remote_copy(
            send2.at[p], recv2.at[p, unit, mp], s2.at[p, u, j], r2.at[p, unit, mp],
            device_id={"seq": first + u, "mp": j}, device_id_type=MESH,
        )

    others = sorted(range(1, M), key=lambda o: abs(o - M // 2))
    near = [(v, o) for v in range(PAIR - 1, -1, -1) for o in others] + [(v, 0) for v in range(1, PAIR)]
    near = [(lax.rem(unit + v, PAIR), lax.rem(mp + o, M)) for v, o in near]
    for p in range(HALVES):
        send2[p] = dot(flat, wout[:, p * half : (p + 1) * half])[:team].astype(BF16)
        for u, j in near:
            copy2(p, u, j).start()
        recv2[p, unit, mp] = send2[p]
    pick = (
        (iota((8, rows), 1) == first * own + iota((8, rows), 0))
        & (iota((8, rows), 0) < team)
    ).astype(F32).astype(BF16)
    mine_x = dot(pick, x.astype(BF16))

    def landed2(p, u, j):
        return pltpu.make_async_remote_copy(
            send2.at[p], recv2.at[p, u, j], s2.at[p, u, j], r2.at[p, u, j],
            device_id={"seq": first + u, "mp": j}, device_id_type=MESH,
        )

    lifted = []
    for p in range(HALVES):
        for u, j in near:
            landed2(p, u, j).wait_recv()
        attn = jnp.zeros((team, half), F32)
        for u in range(PAIR):
            for j in range(M):
                attn = attn + recv2[p, u, j].astype(F32)
        lifted.append(lift([attn[i : i + 1] for i in range(team)], half))
    middle = mine_x + jnp.concatenate(lifted, axis=1)
    normed_mid = layer_norm(middle).astype(BF16)
    for j in range(M):
        for u in range(PAIR):
            mids[u, j] = middle[u * own : (u + 1) * own, j * cols : (j + 1) * cols]
    gate_copy.wait()
    gate = dot(normed_mid, wgu[0])
    up_copy.wait()
    up = dot(normed_mid, wgu[1])
    active = (gate / (1.0 + jnp.exp(-gate)) * up).astype(BF16)
    down_copy.wait()

    def copy3(u, j):
        return pltpu.make_async_remote_copy(
            send3.at[u, j], recv3.at[unit, mp], s3.at[u, j], r3.at[unit, mp],
            device_id={"seq": first + u, "mp": j}, device_id_type=MESH,
        )

    def came3(u, j):
        return pltpu.make_async_remote_copy(
            send3.at[u, j], recv3.at[u, j], s3.at[u, j], r3.at[u, j],
            device_id={"seq": first + u, "mp": j}, device_id_type=MESH,
        )

    for o in others + [0]:
        j = lax.rem(mp + o, M)
        block_out = dot(active, wdown[:, pl.ds(pl.multiple_of(j * cols, cols), cols)])
        for u in range(PAIR):
            send3[u, j] = block_out[u * own : (u + 1) * own].astype(BF16)
        for v in range(PAIR - 1, -1, -1):
            if v or o:
                copy3(lax.rem(unit + v, PAIR), j).start()
    recv3[unit, mp] = send3[unit, mp]
    for u, j in near:
        came3(u, j).wait_recv()
    hidden = mids[unit, mp]
    for u in range(PAIR):
        for j in range(M):
            hidden = hidden + recv3[u, j].astype(F32)
    send4[...] = hidden.astype(BF16)

    def copy4(peer):
        return pltpu.make_async_remote_copy(
            send4, recv4.at[me], s4.at[peer], r4.at[me],
            device_id={"seq": peer}, device_id_type=MESH,
        )

    def came4(peer):
        return pltpu.make_async_remote_copy(
            send4, recv4.at[peer], s4.at[peer], r4.at[peer],
            device_id={"seq": peer}, device_id_type=MESH,
        )

    each(S - 1, lambda o: copy4(lax.rem(me + 1 + o, S)).start())
    recv4[me] = send4[...]
    each(S - 1, lambda o: came4(lax.rem(me + 1 + o, S)).wait_recv())
    for i in range(S):
        hf[i * own : (i + 1) * own, :] = recv4[i].astype(F32)
    emit(hf, h_out)

    each(S - 1, lambda o: copy1(lax.rem(me + 1 + o, S)).wait_send())
    for p in range(HALVES):
        for u, j in near:
            copy2(p, u, j).wait_send()
    for u, j in near:
        copy3(u, j).wait_send()
    each(S - 1, lambda o: copy4(lax.rem(me + 1 + o, S)).wait_send())


def deliver(*refs):
    sems = refs[-1]
    count = len(refs) // 2
    copies = [
        pltpu.make_async_copy(refs[i], refs[count + i], sems.at[i]) for i in range(count)
    ]
    for copy in copies:
        copy.start()
    for copy in copies:
        copy.wait()


def per_device(S, M, inputs, w_qkv, w_out, w_gate_up, w_down, cache_keys, cache_values, lengths):
    batch, steps, width = inputs.shape
    rows = batch * steps
    cols = w_qkv.shape[2]
    heads = cols // DH
    own = rows // S
    pack = own * heads
    team = own * PAIR
    units = w_down.shape[0] // PAIR
    anywhere = pl.BlockSpec(memory_space=pl.ANY)
    vmem = pl.BlockSpec(memory_space=pltpu.VMEM)
    shape = (batch, steps, cols)
    small = pltpu.VMEM((rows, cols), F32)
    dma = pltpu.SemaphoreType.DMA
    results = pl.pallas_call(
        functools.partial(kernel, S, M),
        out_shape=[pltpu.VMEM(shape, BF16)] * 4,
        in_specs=[anywhere] * 8,
        out_specs=[vmem] * 4,
        scratch_shapes=[
            pltpu.SMEM(lengths.shape, jnp.int32),
            pltpu.VMEM(inputs.shape, BF16),
            small,
            small,
            small,
            small,
            pltpu.VMEM((S, pack, cols), F32),
            pltpu.VMEM(w_qkv.shape, BF16),
            pltpu.VMEM((cols // PAIR, width), BF16),
            pltpu.VMEM((2, width, units), BF16),
            pltpu.VMEM((units, width), BF16),
            pltpu.VMEM(cache_keys.shape, BF16),
            pltpu.VMEM(cache_values.shape, BF16),
            pltpu.VMEM((rows, width), F32),
            pltpu.VMEM((S, pack, 2 * DH), BF16),
            pltpu.VMEM((S, pack, 2 * DH), BF16),
            pltpu.VMEM((HALVES, team, width // HALVES), BF16),
            pltpu.VMEM((HALVES, PAIR, M, team, width // HALVES), BF16),
            pltpu.VMEM((PAIR, M, own, cols), BF16),
            pltpu.VMEM((PAIR, M, own, cols), BF16),
            pltpu.VMEM((PAIR, M, own, cols), F32),
            pltpu.VMEM((own, cols), BF16),
            pltpu.VMEM((S, own, cols), BF16),
            dma((2,)),
            dma((3, QKV_CUTS)),
            dma((4,)),
            dma((2,)),
            dma((S,)),
            dma((S,)),
            dma((HALVES, PAIR, M)),
            dma((HALVES, PAIR, M)),
            dma((PAIR, M)),
            dma((PAIR, M)),
            dma((S,)),
            dma((S,)),
        ],
        compiler_params=pltpu.CompilerParams(
            collective_id=0, has_side_effects=True, vmem_limit_bytes=60 * 1024 * 1024
        ),
        name="layer",
    )(lengths, inputs, w_qkv, w_out, w_gate_up, w_down, cache_keys, cache_values)
    queries, keys, values, hidden = (
        pltpu.with_memory_space_constraint(a, pltpu.VMEM) for a in results
    )
    return tuple(
        pl.pallas_call(
            deliver,
            out_shape=[jax.ShapeDtypeStruct(shape, BF16)] * 4,
            in_specs=[vmem] * 4,
            out_specs=[anywhere] * 4,
            scratch_shapes=[dma((4,))],
            name="deliver",
        )(hidden, queries, keys, values)
    )


def solution(mesh):
    cut = P(None, None, "mp")
    cache = P(None, "seq", "mp")
    return jax.shard_map(
        functools.partial(per_device, mesh.shape["seq"], mesh.shape["mp"]),
        mesh=mesh,
        in_specs=(P(), cut, P("mp", None), cut, P("mp", None), cache, cache, P()),
        out_specs=(cut,) * 4,
        check_vma=False,
    )
```

```python
import functools
import math

import jax
import jax.numpy as jnp
from jax import lax
from jax.experimental import pallas as pl
from jax.experimental.pallas import tpu as pltpu
from jax.sharding import PartitionSpec as P

DH = 128
NEG = -1e30
EPS = 1e-05
BASE = 10000.0
MESH = pl.DeviceIdType.MESH
F32 = jnp.float32
BF16 = jnp.bfloat16
QKV_CUTS = 4
HALVES = 2
PAIR = 2


def each(count, body):
    if count <= 8:
        for i in range(count):
            body(i)
    else:
        lax.fori_loop(0, count, lambda i, c: (body(i), c)[1], 0)


def iota(shape, axis):
    return lax.broadcasted_iota(jnp.int32, shape, axis)


def over(value, by):
    return value >> (by.bit_length() - 1) if by & (by - 1) == 0 else lax.div(value, by)


def mod(value, by):
    return value & (by - 1) if by & (by - 1) == 0 else lax.rem(value, by)


def layer_norm(values):
    average = jnp.mean(values, axis=-1, keepdims=True)
    centred = values - average
    variance = jnp.mean(centred * centred, axis=-1, keepdims=True)
    return centred * lax.rsqrt(variance + EPS)


def split3(value):
    high = value.astype(BF16).astype(F32)
    middle = (value - high).astype(BF16).astype(F32)
    return [high, middle, value - high - middle]


def dot(a, b):
    return jnp.dot(a, b, preferred_element_type=F32)


def kernel(
    S, M,
    len_hbm, x_hbm, wqkv_hbm, wout_hbm, wgu_hbm, wdown_hbm, ck_hbm, cv_hbm,
    q_out, k_out, v_out, h_out,
    len_ref, x_in, qf, kf, vf, hf, wides, wqkv, wout, wgu, wdown, ck, cv,
    xf, send1, recv1, send2, recv2, send3, recv3, mids,
    xsem, qsem, wsem, csem, s1, r1, s2, r2, s3, r3,
):
    batch, steps, width = x_in.shape
    rows = batch * steps
    block = ck.shape[1]
    cols = wqkv.shape[2]
    heads = cols // DH
    own = rows // S
    pack = own * heads
    team = own * PAIR
    few = heads // PAIR
    hidden_units = wdown.shape[0]
    me = lax.axis_index("seq")
    mp = lax.axis_index("mp")
    unit = lax.rem(me, PAIR)
    first = me - unit

    x_copy = pltpu.make_async_copy(x_hbm, x_in, xsem.at[0])
    len_copy = pltpu.make_async_copy(len_hbm, len_ref, xsem.at[1])
    len_copy.start()
    x_copy.start()
    cut = width // QKV_CUTS
    q_copies = [
        [
            pltpu.make_async_copy(
                wqkv_hbm.at[j, pl.ds(c * cut, cut)], wqkv.at[j, pl.ds(c * cut, cut)], qsem.at[j, c]
            )
            for c in range(QKV_CUTS)
        ]
        for j in range(3)
    ]
    for c in range(QKV_CUTS):
        q_copies[0][c].start()
    ck_copy = pltpu.make_async_copy(ck_hbm, ck, csem.at[0])
    cv_copy = pltpu.make_async_copy(cv_hbm, cv, csem.at[1])
    ck_copy.start()
    cv_copy.start()
    unit_cols = pl.ds(pl.multiple_of(unit * hidden_units, hidden_units), hidden_units)
    out_copy = pltpu.make_async_copy(
        wout_hbm.at[pl.ds(unit * few * DH, few * DH)], wout, wsem.at[0])
    gate_copy = pltpu.make_async_copy(
        wgu_hbm.at[0, :, unit_cols], wgu.at[0], wsem.at[1])
    up_copy = pltpu.make_async_copy(
        wgu_hbm.at[1, :, unit_cols], wgu.at[1], wsem.at[2])
    down_copy = pltpu.make_async_copy(
        wdown_hbm.at[pl.ds(unit * hidden_units, hidden_units)], wdown, wsem.at[3])

    barrier = pltpu.get_barrier_semaphore()

    def greet(o):
        at = lax.rem(me * M + mp + 1 + o, S * M)
        pl.semaphore_signal(
            barrier, inc=1, device_id={"seq": at // M, "mp": lax.rem(at, M)}, device_id_type=MESH
        )

    if S * M <= 32:
        for o in range(S * M - 1):
            greet(o)
    else:
        each(S * M - 1, greet)

    len_copy.wait()
    token = iota((rows, DH), 0)
    position = mod(token, steps)
    for r in range(batch):
        position = position + jnp.where(over(token, steps) == r, len_ref[r], 0)
    lane = iota((rows, DH), 1)
    fold = mod(lane, DH // 2).astype(F32)
    angle = position.astype(F32) * jnp.exp(fold * (-2.0 * math.log(BASE) / DH))
    cos = jnp.cos(angle)
    sin = jnp.sin(angle)
    sin = jnp.where(lane < DH // 2, -sin, sin)

    x_copy.wait()
    for r in range(batch):
        xf[r * steps : (r + 1) * steps, :] = x_in[r].astype(F32)
    x = xf[...]
    normed = layer_norm(x).astype(BF16)

    def project(j):
        total = None
        for c in range(QKV_CUTS):
            q_copies[j][c].wait()
            if j == 0:
                q_copies[1][c].start()
                q_copies[2][c].start()
            term = dot(normed[:, c * cut : (c + 1) * cut], wqkv[j, c * cut : (c + 1) * cut, :])
            total = term if total is None else total + term
        return total

    def rope(values, ref):
        for h in range(heads):
            v = values[:, h * DH : (h + 1) * DH]
            turned = pltpu.roll(v, DH // 2, 1)
            ref[:, h * DH : (h + 1) * DH] = (v * cos + turned * sin).astype(BF16).astype(F32)

    def emit(ref, out):
        for r in range(batch):
            out[r] = ref[r * steps : (r + 1) * steps, :].astype(BF16)

    rope(project(0), qf)

    full = rows * heads

    def token_of(row):
        return over(row, PAIR * pack) * team + over(mod(row, pack), few)

    def head_of(row):
        return mod(over(row, pack), PAIR) * few + mod(row, few)

    spread = (token_of(iota((full, 1), 0)) == iota((full, rows), 1)).astype(F32).astype(BF16)
    wide = dot(spread, qf[...].astype(BF16))
    own_cols = over(iota((full, cols), 1), DH) == head_of(iota((full, 1), 0))
    wide = jnp.where(own_cols, wide, 0.0)
    wides[...] = wide.reshape(S, pack, cols)
    wide = wide.astype(BF16)

    nt = (((1,), (1,)), ((), ()))
    scale = DH ** -0.5
    group = steps * heads
    ck_copy.wait()
    out_copy.start()
    parts = []
    for r in range(batch):
        raw = lax.dot_general(
            wide[r * group : (r + 1) * group], ck[r], nt, preferred_element_type=F32
        )
        place = iota((group, block), 1) + me * block
        parts.append(jnp.where(place < len_ref[r], raw * scale, NEG))
    scores = jnp.concatenate(parts, axis=0)
    top = jnp.max(scores, axis=1, keepdims=True)
    weights = jnp.where(scores > 0.5 * NEG, jnp.exp(scores - top), 0.0)
    total = jnp.sum(weights, axis=1, keepdims=True)
    cv_copy.wait()
    gate_copy.start()
    weights = weights.astype(BF16)
    summed = jnp.concatenate(
        [dot(weights[r * group : (r + 1) * group], cv[r]) for r in range(batch)], axis=0
    )

    def by_head(wide_rows, start):
        head = head_of(start + iota((wide_rows.shape[0], 1), 0))
        out = jnp.zeros((wide_rows.shape[0], DH), F32)
        for h in range(heads):
            out = out + jnp.where(head == h, wide_rows[:, h * DH : (h + 1) * DH], 0.0)
        return out

    spot = iota((full, DH), 1)
    stats = jnp.zeros((full, DH), F32)
    for i, piece in enumerate(split3(top) + split3(total)):
        stats = jnp.where(spot == i, piece, stats)
    send1[:, :, :DH] = by_head(summed, 0).reshape(S, pack, DH).astype(BF16)
    send1[:, :, DH:] = stats.reshape(S, pack, DH).astype(BF16)

    pl.semaphore_wait(barrier, S * M - 1)

    def copy1(peer):
        return pltpu.make_async_remote_copy(
            send1.at[peer], recv1.at[me], s1.at[peer], r1.at[me],
            device_id={"seq": peer}, device_id_type=MESH,
        )

    def came(buf, src, send_sem, recv_sem, slot, axis):
        return pltpu.make_async_remote_copy(
            src, buf.at[slot], send_sem, recv_sem.at[slot],
            device_id={axis: slot}, device_id_type=MESH,
        )

    each(S - 1, lambda o: copy1(lax.rem(me + 1 + o, S)).start())
    recv1[me] = send1[me]

    up_copy.start()
    keys = project(1)
    down_copy.start()
    rope(keys, kf)
    values = project(2)
    vf[...] = values.astype(BF16).astype(F32)
    fresh = (
        lax.dot_general(
            wides[me].astype(BF16), kf[...].astype(BF16), nt, preferred_element_type=F32
        )
        * scale
    )
    row = token_of(me * pack + iota((pack, 1), 0))
    col = iota((pack, rows), 1)
    live = (over(row, steps) == over(col, steps)) & (col <= row)
    fresh = jnp.where(live, fresh, NEG)
    fresh_top = jnp.max(fresh, axis=1, keepdims=True)
    fresh_w = jnp.where(live, jnp.exp(fresh - fresh_top), 0.0)
    fresh_total = jnp.sum(fresh_w, axis=1, keepdims=True)
    fresh_sum = by_head(dot(fresh_w.astype(BF16), vf[...].astype(BF16)), me * pack)

    def wait1(o):
        peer = lax.rem(me + 1 + o, S)
        came(recv1, send1.at[peer], s1.at[peer], r1, peer, "seq").wait_recv()

    each(S - 1, wait1)
    stats = recv1[:, :, DH:].astype(F32)
    tops = stats[:, :, 0:1] + stats[:, :, 1:2] + stats[:, :, 2:3]
    sums = stats[:, :, 3:4] + stats[:, :, 4:5] + stats[:, :, 5:6]
    high = jnp.maximum(jnp.max(tops, axis=0), fresh_top)
    shrink = jnp.exp(tops - high[None])
    fresh_shrink = jnp.exp(fresh_top - high)
    whole = jnp.sum(sums * shrink, axis=0) + fresh_total * fresh_shrink
    context = jnp.sum(recv1[:, :, :DH].astype(F32) * shrink, axis=0) + fresh_sum * fresh_shrink
    context = context / whole
    context = context.astype(BF16).astype(F32)
    part_cols = few * DH
    own_cols = over(iota((pack, part_cols), 1), DH) == mod(iota((pack, 1), 0), few)
    tiled = jnp.where(own_cols, jnp.concatenate([context] * few, axis=1), 0.0)

    def lift(pieces, columns):
        at = iota((8, columns), 0)
        out = jnp.zeros((8, columns), F32)
        for i, piece in enumerate(pieces):
            out = jnp.where(at == i, piece, out)
        return out

    tiled_row = over(iota((pack, part_cols), 0), few)
    flat = lift(
        [
            jnp.sum(jnp.where(tiled_row == i, tiled, 0.0), axis=0, keepdims=True)
            for i in range(team)
        ],
        part_cols,
    ).astype(BF16)
    out_copy.wait()
    half = width // HALVES

    def copy2(p, u, j):
        return pltpu.make_async_remote_copy(
            send2.at[p], recv2.at[p, unit, mp], s2.at[p, u, j], r2.at[p, unit, mp],
            device_id={"seq": first + u, "mp": j}, device_id_type=MESH,
        )

    others = sorted(range(1, M), key=lambda o: abs(o - M // 2))
    near = [(v, o) for v in range(PAIR - 1, -1, -1) for o in others] + [(v, 0) for v in range(1, PAIR)]
    near = [(lax.rem(unit + v, PAIR), lax.rem(mp + o, M)) for v, o in near]
    for p in range(HALVES):
        send2[p] = dot(flat, wout[:, p * half : (p + 1) * half])[:team].astype(BF16)
        for u, j in near:
            copy2(p, u, j).start()
        recv2[p, unit, mp] = send2[p]
    pick = (
        (iota((8, rows), 1) == first * own + iota((8, rows), 0))
        & (iota((8, rows), 0) < team)
    ).astype(F32).astype(BF16)
    mine_x = dot(pick, x.astype(BF16))

    def landed2(p, u, j):
        return pltpu.make_async_remote_copy(
            send2.at[p], recv2.at[p, u, j], s2.at[p, u, j], r2.at[p, u, j],
            device_id={"seq": first + u, "mp": j}, device_id_type=MESH,
        )

    lifted = []
    for p in range(HALVES):
        for u, j in near:
            landed2(p, u, j).wait_recv()
        attn = jnp.zeros((team, half), F32)
        for u in range(PAIR):
            for j in range(M):
                attn = attn + recv2[p, u, j].astype(F32)
        lifted.append(lift([attn[i : i + 1] for i in range(team)], half))
    middle = mine_x + jnp.concatenate(lifted, axis=1)
    normed_mid = layer_norm(middle).astype(BF16)
    for j in range(M):
        mids[j] = jnp.where(unit == 0, middle[:team, j * cols : (j + 1) * cols], 0.0)
    gate_copy.wait()
    gate = dot(normed_mid, wgu[0])
    up_copy.wait()
    up = dot(normed_mid, wgu[1])
    active = (gate / (1.0 + jnp.exp(-gate)) * up).astype(BF16)
    down_copy.wait()

    def copy3(seq, j):
        return pltpu.make_async_remote_copy(
            send3.at[j], recv3.at[me, mp], s3.at[seq, j], r3.at[me, mp],
            device_id={"seq": seq, "mp": j}, device_id_type=MESH,
        )

    def came3(seq, j):
        return pltpu.make_async_remote_copy(
            send3.at[j], recv3.at[seq, j], s3.at[seq, j], r3.at[seq, j],
            device_id={"seq": seq, "mp": j}, device_id_type=MESH,
        )

    def down_block(j):
        return dot(active, wdown[:, pl.ds(pl.multiple_of(j * cols, cols), cols)])[:team]

    def all_blocks(act):
        for o in others:
            j = lax.rem(mp + o, M)
            each(S, lambda i: act(lax.rem(me + S // 2 + i, S), j))
        each(S - 1, lambda i: act(lax.rem(me + 1 + i, S), mp))

    for o in others:
        j = lax.rem(mp + o, M)
        send3[j] = down_block(j).astype(BF16)
        each(S, lambda i: copy3(lax.rem(me + S // 2 + i, S), j).start())
    send3[mp] = (down_block(mp) + mids[mp]).astype(BF16)
    each(S - 1, lambda i: copy3(lax.rem(me + 1 + i, S), mp).start())
    recv3[me, mp] = send3[mp]
    emit(qf, q_out)
    emit(kf, k_out)
    emit(vf, v_out)
    all_blocks(lambda seq, j: came3(seq, j).wait_recv())
    for i in range(S // PAIR):
        hidden = jnp.zeros((team, cols), F32)
        for u in range(PAIR):
            for j in range(M):
                hidden = hidden + recv3[i * PAIR + u, j].astype(F32)
        hf[i * team : (i + 1) * team, :] = hidden
    emit(hf, h_out)

    each(S - 1, lambda o: copy1(lax.rem(me + 1 + o, S)).wait_send())
    for p in range(HALVES):
        for u, j in near:
            copy2(p, u, j).wait_send()
    all_blocks(lambda seq, j: copy3(seq, j).wait_send())


def deliver(*refs):
    sems = refs[-1]
    count = len(refs) // 2
    copies = [
        pltpu.make_async_copy(refs[i], refs[count + i], sems.at[i]) for i in range(count)
    ]
    for copy in copies:
        copy.start()
    for copy in copies:
        copy.wait()


def per_device(S, M, inputs, w_qkv, w_out, w_gate_up, w_down, cache_keys, cache_values, lengths):
    batch, steps, width = inputs.shape
    rows = batch * steps
    cols = w_qkv.shape[2]
    heads = cols // DH
    own = rows // S
    pack = own * heads
    team = own * PAIR
    units = w_down.shape[0] // PAIR
    anywhere = pl.BlockSpec(memory_space=pl.ANY)
    vmem = pl.BlockSpec(memory_space=pltpu.VMEM)
    shape = (batch, steps, cols)
    small = pltpu.VMEM((rows, cols), F32)
    dma = pltpu.SemaphoreType.DMA
    results = pl.pallas_call(
        functools.partial(kernel, S, M),
        out_shape=[pltpu.VMEM(shape, BF16)] * 4,
        in_specs=[anywhere] * 8,
        out_specs=[vmem] * 4,
        scratch_shapes=[
            pltpu.SMEM(lengths.shape, jnp.int32),
            pltpu.VMEM(inputs.shape, BF16),
            small,
            small,
            small,
            small,
            pltpu.VMEM((S, pack, cols), F32),
            pltpu.VMEM(w_qkv.shape, BF16),
            pltpu.VMEM((cols // PAIR, width), BF16),
            pltpu.VMEM((2, width, units), BF16),
            pltpu.VMEM((units, width), BF16),
            pltpu.VMEM(cache_keys.shape, BF16),
            pltpu.VMEM(cache_values.shape, BF16),
            pltpu.VMEM((rows, width), F32),
            pltpu.VMEM((S, pack, 2 * DH), BF16),
            pltpu.VMEM((S, pack, 2 * DH), BF16),
            pltpu.VMEM((HALVES, team, width // HALVES), BF16),
            pltpu.VMEM((HALVES, PAIR, M, team, width // HALVES), BF16),
            pltpu.VMEM((M, team, cols), BF16),
            pltpu.VMEM((S, M, team, cols), BF16),
            pltpu.VMEM((M, team, cols), F32),
            dma((2,)),
            dma((3, QKV_CUTS)),
            dma((4,)),
            dma((2,)),
            dma((S,)),
            dma((S,)),
            dma((HALVES, PAIR, M)),
            dma((HALVES, PAIR, M)),
            dma((S, M)),
            dma((S, M)),
        ],
        compiler_params=pltpu.CompilerParams(
            collective_id=0, has_side_effects=True, vmem_limit_bytes=60 * 1024 * 1024
        ),
        name="layer",
    )(lengths, inputs, w_qkv, w_out, w_gate_up, w_down, cache_keys, cache_values)
    queries, keys, values, hidden = (
        pltpu.with_memory_space_constraint(a, pltpu.VMEM) for a in results
    )
    return tuple(
        pl.pallas_call(
            deliver,
            out_shape=[jax.ShapeDtypeStruct(shape, BF16)] * 4,
            in_specs=[vmem] * 4,
            out_specs=[anywhere] * 4,
            scratch_shapes=[dma((4,))],
            name="deliver",
        )(hidden, queries, keys, values)
    )


def solution(mesh):
    cut = P(None, None, "mp")
    cache = P(None, "seq", "mp")
    return jax.shard_map(
        functools.partial(per_device, mesh.shape["seq"], mesh.shape["mp"]),
        mesh=mesh,
        in_specs=(P(), cut, P("mp", None), cut, P("mp", None), cache, cache, P()),
        out_specs=(cut,) * 4,
        check_vma=False,
    )
```

```python
import functools
import math

import jax
import jax.numpy as jnp
from jax import lax
from jax.experimental import pallas as pl
from jax.experimental.pallas import tpu as pltpu
from jax.sharding import PartitionSpec as P

DH = 128
NEG = -1e30
EPS = 1e-05
BASE = 10000.0
MESH = pl.DeviceIdType.MESH
F32 = jnp.float32
BF16 = jnp.bfloat16
QKV_CUTS = 4
HALVES = 2


def each(count, body):
    if count <= 8:
        for i in range(count):
            body(i)
    else:
        lax.fori_loop(0, count, lambda i, c: (body(i), c)[1], 0)


def iota(shape, axis):
    return lax.broadcasted_iota(jnp.int32, shape, axis)


def far_first(me, count):
    if count > 8 or count & (count - 1):
        return None
    order = []
    for k in range(count - 1, -1, -1):
        peer, bit = me, 1
        while bit < count:
            if k & bit:
                peer = peer + bit * (1 - 2 * lax.rem(me // bit, 2))
            bit *= 2
        order.append(peer)
    return order


def layer_norm(values):
    average = jnp.mean(values, axis=-1, keepdims=True)
    centred = values - average
    variance = jnp.mean(centred * centred, axis=-1, keepdims=True)
    return centred * lax.rsqrt(variance + EPS)


def split3(value):
    high = value.astype(BF16).astype(F32)
    middle = (value - high).astype(BF16).astype(F32)
    return [high, middle, value - high - middle]


def dot(a, b):
    return jnp.dot(a, b, preferred_element_type=F32)


def kernel(
    S, M,
    len_hbm, x_hbm, wqkv_hbm, wout_hbm, wgu_hbm, wdown_hbm, ck_hbm, cv_hbm,
    q_out, k_out, v_out, h_out,
    len_ref, x_in, qf, kf, vf, hf, wides, wqkv, wout, wgu, wdown, ck, cv,
    xf, send1, recv1, send2, recv2, send3, recv3, mids,
    xsem, qsem, wsem, csem, s1, r1, s2, r2, s3, r3,
):
    batch, steps, width = x_in.shape
    rows = batch * steps
    block = ck.shape[1]
    cols = wqkv.shape[2]
    heads = cols // DH
    own = rows // S
    pack = own * heads
    me = lax.axis_index("seq")
    mp = lax.axis_index("mp")

    order = far_first(me, S)

    def to_seq(act, me_too):
        count = S if me_too else S - 1
        if order is None:
            each(count, lambda i: act(lax.rem(me + 1 + i, S)))
        else:
            for peer in order[:count]:
                act(peer)

    x_copy = pltpu.make_async_copy(x_hbm, x_in, xsem.at[0])
    len_copy = pltpu.make_async_copy(len_hbm, len_ref, xsem.at[1])
    x_copy.start()
    len_copy.start()
    cut = width // QKV_CUTS
    q_copies = [
        [
            pltpu.make_async_copy(
                wqkv_hbm.at[j, pl.ds(c * cut, cut)], wqkv.at[j, pl.ds(c * cut, cut)], qsem.at[j, c]
            )
            for c in range(QKV_CUTS)
        ]
        for j in range(3)
    ]
    for c in range(QKV_CUTS):
        q_copies[0][c].start()
    ck_copy = pltpu.make_async_copy(ck_hbm, ck, csem.at[0])
    cv_copy = pltpu.make_async_copy(cv_hbm, cv, csem.at[1])
    ck_copy.start()
    cv_copy.start()
    out_copy = pltpu.make_async_copy(wout_hbm, wout, wsem.at[0])
    gate_copy = pltpu.make_async_copy(wgu_hbm.at[0], wgu.at[0], wsem.at[1])
    up_copy = pltpu.make_async_copy(wgu_hbm.at[1], wgu.at[1], wsem.at[2])
    down_copy = pltpu.make_async_copy(wdown_hbm, wdown, wsem.at[3])

    barrier = pltpu.get_barrier_semaphore()

    def greet(o):
        at = lax.rem(me * M + mp + 1 + o, S * M)
        pl.semaphore_signal(
            barrier, inc=1, device_id={"seq": at // M, "mp": lax.rem(at, M)}, device_id_type=MESH
        )

    if S * M <= 32:
        for o in range(S * M - 1):
            greet(o)
    else:
        each(S * M - 1, greet)

    x_copy.wait()
    for r in range(batch):
        xf[r * steps : (r + 1) * steps, :] = x_in[r].astype(F32)
    x = xf[...]
    normed = layer_norm(x).astype(BF16)

    def project(j):
        total = None
        for c in range(QKV_CUTS):
            q_copies[j][c].wait()
            if j == 0:
                q_copies[1][c].start()
                q_copies[2][c].start()
            term = dot(normed[:, c * cut : (c + 1) * cut], wqkv[j, c * cut : (c + 1) * cut, :])
            total = term if total is None else total + term
        return total

    len_copy.wait()
    token = iota((rows, DH), 0)
    position = lax.rem(token, steps)
    for r in range(batch):
        position = position + jnp.where(token // steps == r, len_ref[r], 0)
    lane = iota((rows, DH), 1)
    fold = lax.rem(lane, DH // 2).astype(F32)
    angle = position.astype(F32) * jnp.exp(fold * (-2.0 * math.log(BASE) / DH))
    cos = jnp.cos(angle)
    sin = jnp.sin(angle)
    sin = jnp.where(lane < DH // 2, -sin, sin)

    def rope(values, ref):
        for h in range(heads):
            v = values[:, h * DH : (h + 1) * DH]
            turned = pltpu.roll(v, DH // 2, 1)
            ref[:, h * DH : (h + 1) * DH] = (v * cos + turned * sin).astype(BF16).astype(F32)

    def emit(ref, out):
        for r in range(batch):
            out[r] = ref[r * steps : (r + 1) * steps, :].astype(BF16)

    rope(project(0), qf)

    full = rows * heads
    spread = (iota((full, rows), 0) // heads == iota((full, rows), 1)).astype(F32).astype(BF16)
    wide = dot(spread, qf[...].astype(BF16))
    own_cols = iota((full, cols), 1) // DH == lax.rem(iota((full, cols), 0), heads)
    wide = jnp.where(own_cols, wide, 0.0)
    wides[...] = wide.reshape(S, pack, cols)
    wide = wide.astype(BF16)

    nt = (((1,), (1,)), ((), ()))
    scale = DH ** -0.5
    group = steps * heads
    ck_copy.wait()
    out_copy.start()
    parts = []
    for r in range(batch):
        raw = lax.dot_general(
            wide[r * group : (r + 1) * group], ck[r], nt, preferred_element_type=F32
        )
        place = iota((group, block), 1) + me * block
        parts.append(jnp.where(place < len_ref[r], raw * scale, NEG))
    scores = jnp.concatenate(parts, axis=0)
    top = jnp.max(scores, axis=1, keepdims=True)
    weights = jnp.where(scores > 0.5 * NEG, jnp.exp(scores - top), 0.0)
    total = jnp.sum(weights, axis=1, keepdims=True)
    cv_copy.wait()
    gate_copy.start()
    weights = weights.astype(BF16)
    summed = jnp.concatenate(
        [dot(weights[r * group : (r + 1) * group], cv[r]) for r in range(batch)], axis=0
    )

    def by_head(wide_rows):
        head_of = lax.rem(iota((wide_rows.shape[0], DH), 0), heads)
        out = jnp.zeros((wide_rows.shape[0], DH), F32)
        for h in range(heads):
            out = out + jnp.where(head_of == h, wide_rows[:, h * DH : (h + 1) * DH], 0.0)
        return out

    spot = iota((full, DH), 1)
    stats = jnp.zeros((full, DH), F32)
    for i, piece in enumerate(split3(top) + split3(total)):
        stats = jnp.where(spot == i, piece, stats)
    send1[:, :, :DH] = by_head(summed).reshape(S, pack, DH).astype(BF16)
    send1[:, :, DH:] = stats.reshape(S, pack, DH).astype(BF16)

    pl.semaphore_wait(barrier, S * M - 1)

    def copy1(peer):
        return pltpu.make_async_remote_copy(
            send1.at[peer], recv1.at[me], s1.at[peer], r1.at[me],
            device_id={"seq": peer}, device_id_type=MESH,
        )

    def came(buf, src, send_sem, recv_sem, slot, axis):
        return pltpu.make_async_remote_copy(
            src, buf.at[slot], send_sem, recv_sem.at[slot],
            device_id={axis: slot}, device_id_type=MESH,
        )

    to_seq(lambda peer: copy1(peer).start(), False)
    recv1[me] = send1[me]

    up_copy.start()
    keys = project(1)
    down_copy.start()
    rope(keys, kf)
    values = project(2)
    vf[...] = values.astype(BF16).astype(F32)
    fresh = (
        lax.dot_general(
            wides[me].astype(BF16), kf[...].astype(BF16), nt, preferred_element_type=F32
        )
        * scale
    )
    row = me * pack + iota((pack, rows), 0)
    col = iota((pack, rows), 1)
    live = (row // group == col // steps) & (lax.rem(col, steps) <= lax.rem(row // heads, steps))
    fresh = jnp.where(live, fresh, NEG)
    fresh_top = jnp.max(fresh, axis=1, keepdims=True)
    fresh_w = jnp.where(live, jnp.exp(fresh - fresh_top), 0.0)
    fresh_total = jnp.sum(fresh_w, axis=1, keepdims=True)
    fresh_sum = by_head(dot(fresh_w.astype(BF16), vf[...].astype(BF16)))
    emit(qf, q_out)
    emit(kf, k_out)
    emit(vf, v_out)

    def wait1(o):
        peer = lax.rem(me + 1 + o, S)
        came(recv1, send1.at[peer], s1.at[peer], r1, peer, "seq").wait_recv()

    each(S - 1, wait1)
    stats = recv1[:, :, DH:].astype(F32)
    tops = stats[:, :, 0:1] + stats[:, :, 1:2] + stats[:, :, 2:3]
    sums = stats[:, :, 3:4] + stats[:, :, 4:5] + stats[:, :, 5:6]
    high = jnp.maximum(jnp.max(tops, axis=0), fresh_top)
    shrink = jnp.exp(tops - high[None])
    fresh_shrink = jnp.exp(fresh_top - high)
    whole = jnp.sum(sums * shrink, axis=0) + fresh_total * fresh_shrink
    context = jnp.sum(recv1[:, :, :DH].astype(F32) * shrink, axis=0) + fresh_sum * fresh_shrink
    context = context / whole
    context = context.astype(BF16).astype(F32)
    own_cols = iota((pack, cols), 1) // DH == lax.rem(iota((pack, cols), 0), heads)
    tiled = jnp.where(own_cols, jnp.concatenate([context] * heads, axis=1), 0.0)

    def lift(pieces, columns):
        at = iota((8, columns), 0)
        out = jnp.zeros((8, columns), F32)
        for i, piece in enumerate(pieces):
            out = jnp.where(at == i, piece, out)
        return out

    tiled_row = iota((pack, cols), 0) // heads
    flat = lift(
        [
            jnp.sum(jnp.where(tiled_row == i, tiled, 0.0), axis=0, keepdims=True)
            for i in range(own)
        ],
        cols,
    ).astype(BF16)
    out_copy.wait()
    half = width // HALVES

    def copy2(p, peer):
        return pltpu.make_async_remote_copy(
            send2.at[p], recv2.at[p, mp], s2.at[p, peer], r2.at[p, mp],
            device_id={"mp": peer}, device_id_type=MESH,
        )

    others = sorted(range(1, M), key=lambda o: abs(o - M // 2))
    for p in range(HALVES):
        send2[p] = dot(flat, wout[:, p * half : (p + 1) * half])[:own].astype(BF16)
        for o in others:
            copy2(p, lax.rem(mp + o, M)).start()
        recv2[p, mp] = send2[p]
    pick = (
        (iota((8, rows), 1) == me * own + iota((8, rows), 0)) & (iota((8, rows), 0) < own)
    ).astype(F32).astype(BF16)
    mine_x = dot(pick, x.astype(BF16))

    def landed2(p, peer):
        return pltpu.make_async_remote_copy(
            send2.at[p], recv2.at[p, peer], s2.at[p, peer], r2.at[p, peer],
            device_id={"mp": peer}, device_id_type=MESH,
        )

    lifted = []
    for p in range(HALVES):
        for o in others:
            landed2(p, lax.rem(mp + o, M)).wait_recv()
        attn = recv2[p, 0].astype(F32)
        for j in range(1, M):
            attn = attn + recv2[p, j].astype(F32)
        lifted.append(lift([attn[i : i + 1] for i in range(own)], half))
    middle = mine_x + jnp.concatenate(lifted, axis=1)
    normed_mid = layer_norm(middle).astype(BF16)
    for j in range(M):
        mids[j] = middle[:own, j * cols : (j + 1) * cols]
    gate_copy.wait()
    gate = dot(normed_mid, wgu[0])
    up_copy.wait()
    up = dot(normed_mid, wgu[1])
    active = (gate / (1.0 + jnp.exp(-gate)) * up).astype(BF16)
    down_copy.wait()

    def copy3(seq, j):
        return pltpu.make_async_remote_copy(
            send3.at[j], recv3.at[me, mp], s3.at[seq, j], r3.at[me, mp],
            device_id={"seq": seq, "mp": j}, device_id_type=MESH,
        )

    def came3(seq, j):
        return pltpu.make_async_remote_copy(
            send3.at[j], recv3.at[seq, j], s3.at[seq, j], r3.at[seq, j],
            device_id={"seq": seq, "mp": j}, device_id_type=MESH,
        )

    def down_block(j):
        return dot(active, wdown[:, pl.ds(pl.multiple_of(j * cols, cols), cols)])[:own]

    def all_blocks(act):
        for o in others:
            j = lax.rem(mp + o, M)
            each(S, lambda i: act(lax.rem(me + S // 2 + i, S), j))
        each(S - 1, lambda i: act(lax.rem(me + 1 + i, S), mp))

    for o in others:
        j = lax.rem(mp + o, M)
        send3[j] = down_block(j).astype(BF16)
        to_seq(lambda peer: copy3(peer, j).start(), True)
    send3[mp] = (down_block(mp) + mids[mp]).astype(BF16)
    to_seq(lambda peer: copy3(peer, mp).start(), False)
    recv3[me, mp] = send3[mp]
    all_blocks(lambda seq, j: came3(seq, j).wait_recv())
    for i in range(S):
        hidden = recv3[i, 0].astype(F32)
        for j in range(1, M):
            hidden = hidden + recv3[i, j].astype(F32)
        hf[i * own : (i + 1) * own, :] = hidden
    emit(hf, h_out)

    each(S - 1, lambda o: copy1(lax.rem(me + 1 + o, S)).wait_send())
    for p in range(HALVES):
        for o in others:
            copy2(p, lax.rem(mp + o, M)).wait_send()
    all_blocks(lambda seq, j: copy3(seq, j).wait_send())


def deliver(*refs):
    sems = refs[-1]
    count = len(refs) // 2
    copies = [
        pltpu.make_async_copy(refs[i], refs[count + i], sems.at[i]) for i in range(count)
    ]
    for copy in copies:
        copy.start()
    for copy in copies:
        copy.wait()


def per_device(S, M, inputs, w_qkv, w_out, w_gate_up, w_down, cache_keys, cache_values, lengths):
    batch, steps, width = inputs.shape
    rows = batch * steps
    cols = w_qkv.shape[2]
    heads = cols // DH
    own = rows // S
    pack = own * heads
    anywhere = pl.BlockSpec(memory_space=pl.ANY)
    vmem = pl.BlockSpec(memory_space=pltpu.VMEM)
    shape = (batch, steps, cols)
    small = pltpu.VMEM((rows, cols), F32)
    dma = pltpu.SemaphoreType.DMA
    results = pl.pallas_call(
        functools.partial(kernel, S, M),
        out_shape=[pltpu.VMEM(shape, BF16)] * 4,
        in_specs=[anywhere] * 8,
        out_specs=[vmem] * 4,
        scratch_shapes=[
            pltpu.SMEM(lengths.shape, jnp.int32),
            pltpu.VMEM(inputs.shape, BF16),
            small,
            small,
            small,
            small,
            pltpu.VMEM((S, pack, cols), F32),
            pltpu.VMEM(w_qkv.shape, BF16),
            pltpu.VMEM(w_out.shape, BF16),
            pltpu.VMEM(w_gate_up.shape, BF16),
            pltpu.VMEM(w_down.shape, BF16),
            pltpu.VMEM(cache_keys.shape, BF16),
            pltpu.VMEM(cache_values.shape, BF16),
            pltpu.VMEM((rows, width), F32),
            pltpu.VMEM((S, pack, 2 * DH), BF16),
            pltpu.VMEM((S, pack, 2 * DH), BF16),
            pltpu.VMEM((HALVES, own, width // HALVES), BF16),
            pltpu.VMEM((HALVES, M, own, width // HALVES), BF16),
            pltpu.VMEM((M, own, cols), BF16),
            pltpu.VMEM((S, M, own, cols), BF16),
            pltpu.VMEM((M, own, cols), F32),
            dma((2,)),
            dma((3, QKV_CUTS)),
            dma((4,)),
            dma((2,)),
            dma((S,)),
            dma((S,)),
            dma((HALVES, M)),
            dma((HALVES, M)),
            dma((S, M)),
            dma((S, M)),
        ],
        compiler_params=pltpu.CompilerParams(
            collective_id=0, has_side_effects=True, vmem_limit_bytes=60 * 1024 * 1024
        ),
        name="layer",
    )(lengths, inputs, w_qkv, w_out, w_gate_up, w_down, cache_keys, cache_values)
    queries, keys, values, hidden = (
        pltpu.with_memory_space_constraint(a, pltpu.VMEM) for a in results
    )
    return tuple(
        pl.pallas_call(
            deliver,
            out_shape=[jax.ShapeDtypeStruct(shape, BF16)] * 4,
            in_specs=[vmem] * 4,
            out_specs=[anywhere] * 4,
            scratch_shapes=[dma((4,))],
            name="deliver",
        )(hidden, queries, keys, values)
    )


def solution(mesh):
    cut = P(None, None, "mp")
    cache = P(None, "seq", "mp")
    return jax.shard_map(
        functools.partial(per_device, mesh.shape["seq"], mesh.shape["mp"]),
        mesh=mesh,
        in_specs=(P(), cut, P("mp", None), cut, P("mp", None), cache, cache, P()),
        out_specs=(cut,) * 4,
        check_vma=False,
    )
```
